256 devices in a mesh: row: 32 (over y_hi, z, core), col: 8 (over x, y_lo).
Axes of the slice: x: 4, y: 4 (y_hi: 2, y_lo: 2; y = y_hi * 2 + y_lo), z: 8, core: 2. Of those that a mesh axis runs over, the one named last changes fastest.
Arguments:
- noise_latents: float32 [16384, 4096], P('row', 'col'), may hold values from -6 to 6
- data_latents: float32 [8192, 4096], P('col', 'row'), may hold values from -6 to 6
- flow_times: float32 [16384], P('row'), may hold values from 0 to 1
Outputs:
- velocity: float32 [16384, 4096], P('row', 'col')
- interpolant: float32 [16384, 4096], P('row', 'col')
The draws below stay inside these ranges and needn't reach their ends.
All inputs are finite; a program needn't handle non-finite values.
Results may differ from the reference program's by a relative error of at most 0.0025.
Values may be sent and summed in bfloat16 or wider, within the bound.
A program may use at most 64 MiB of HBM per device.

```python
import math
import jax
import jax.numpy as jnp
from jax import lax

D = 4096
SWEEPS = 3
NOISE_COUNT = 16384
DATA_COUNT = 8192


def level_of(rng, dims, pieces, smallest, top_value):
    def one(axis_at, shards_of):
        heights = jax.random.uniform(jax.random.fold_in(jax.random.fold_in(rng, 6), axis_at), (shards_of,), jnp.float32, smallest / len(pieces), top_value / len(pieces))
        return jnp.repeat(jnp.exp(heights), dims[axis_at] // shards_of).reshape((-1,) + (1,) * (len(dims) - axis_at - 1))

    factor_of = one(*pieces[0])
    for cut in pieces[1:]:
        factor_of = factor_of * one(*cut)
    return factor_of


def gaussian(stream_key, dims, width, limit, split=(), held_as=jnp.bfloat16):
    entries = width * jax.random.normal(stream_key, dims, jnp.float32)
    if split:
        entries = entries * level_of(stream_key, dims, split, -0.22, 0.18)
    return jnp.clip(entries, -limit, limit).astype(held_as)


def setup_inputs(seed: int = 0) -> dict:
    key_of = jax.random.split(jax.random.key(seed), 4)
    noise_latents = gaussian(key_of[0], (NOISE_COUNT, D), 1.0, 6.0, ((0, 32), (1, 8)), jnp.float32)
    data_latents = gaussian(key_of[1], (DATA_COUNT, D), 1.0, 6.0, ((0, 8), (1, 32)), jnp.float32)
    flow_times = jnp.clip(1.0 * jax.random.uniform(key_of[2], (NOISE_COUNT,), jnp.float32) ** level_of(key_of[2], (NOISE_COUNT,), ((0, 32),), -0.2, 0.2), 0.0, 1.0)
    return {"noise_latents": noise_latents, "data_latents": data_latents, "flow_times": flow_times}


entropic_epsilon = 0.02


def stable_logsumexp(scores, axis):
    largest = jnp.max(scores, axis=axis, keepdims=True)
    sums = jnp.sum(jnp.exp(scores - largest), axis=axis)
    return jnp.squeeze(largest, axis) + jnp.log(sums)


def reference(noise_latents, data_latents, flow_times):
    noise_bf = noise_latents.astype(jnp.bfloat16)
    data_bf = data_latents.astype(jnp.bfloat16)
    noise_wide = noise_bf.astype(jnp.float32)
    data_wide = data_bf.astype(jnp.float32)
    sq_noise = jnp.sum(noise_wide * noise_wide, axis=1)
    sq_data = jnp.sum(data_wide * data_wide, axis=1)
    inner = lax.dot_general(noise_bf, data_bf, (((1,), (1,)), ((), ())), preferred_element_type=jnp.float32)
    squared_distance = (sq_noise[:, None] + sq_data[None, :] - 2.0 * inner) / D
    data_potential = jnp.zeros((DATA_COUNT,), jnp.float32)
    for sweep_index in range(SWEEPS):
        noise_potential = -entropic_epsilon * stable_logsumexp((data_potential[None, :] - squared_distance) / entropic_epsilon, 1) - entropic_epsilon * math.log(NOISE_COUNT)
        data_potential = -entropic_epsilon * stable_logsumexp((noise_potential[:, None] - squared_distance) / entropic_epsilon, 0) - entropic_epsilon * math.log(DATA_COUNT)
    noise_potential = -entropic_epsilon * stable_logsumexp((data_potential[None, :] - squared_distance) / entropic_epsilon, 1) - entropic_epsilon * math.log(NOISE_COUNT)
    transport_plan = jnp.exp((noise_potential[:, None] + data_potential[None, :] - squared_distance) / entropic_epsilon).astype(jnp.bfloat16)
    matched = NOISE_COUNT * jnp.dot(transport_plan, data_bf, preferred_element_type=jnp.float32)
    velocity = matched - noise_latents
    interpolant = (1.0 - flow_times)[:, None] * noise_latents + flow_times[:, None] * matched
    return velocity, interpolant
```

```python
import math

import jax
import jax.numpy as jnp
from jax import lax
from jax.experimental import pallas as pl
from jax.experimental.pallas import tpu as pltpu
from jax.sharding import PartitionSpec as P

D = 4096
SWEEPS = 3
entropic_epsilon = 0.02
MESH = pl.DeviceIdType.MESH
LOG2E = 1.0 / math.log(2.0)

ROWS, COLS = 512, 1024
QS, QW = 16, 256
LANES = 128


def log2sumexp2(values):
    largest = jnp.max(values, axis=0, keepdims=True)
    sums = jnp.sum(jnp.exp2(values - largest), axis=0, keepdims=True)
    return largest + jnp.log(sums) * LOG2E


def kernel(noise_ref, data_ref, out_ref,
           nb, db, scores, plan, parts, got, lane_lse, noise_col, data_row, sq_n, sq_d,
           row_x, col_x, pair_x,
           n_send, n_recv, d_send, d_recv, s_send, s_recv,
           rx_send, rx_recv, cx_send, cx_recv, px_send, px_recv, m_send, m_recv):
    row, col = lax.axis_index("row"), lax.axis_index("col")
    yhi, z, core = row // 16, lax.rem(row // 2, 8), lax.rem(row, 2)
    x, ylo = col // 2, lax.rem(col, 2)
    chip = row // 2

    def at_x(shift, other=False):
        return lax.rem(x + shift + 4, 4) * 2 + (1 - ylo if other else ylo)

    def at_z(shift, other=False):
        return (1 - yhi if other else yhi) * 8 + lax.rem(z + shift + 8, 8)

    sibling = (row + 1 - 2 * core, col)

    barrier = pltpu.get_barrier_semaphore()
    pl.semaphore_signal(barrier, inc=1, device_id=sibling, device_id_type=MESH)

    def greet_col(k, _):
        pl.semaphore_signal(barrier, inc=1, device_id=(row, lax.rem(col + k, 8)), device_id_type=MESH)
        return 0

    def greet_row(k, _):
        pl.semaphore_signal(barrier, inc=1, device_id=(lax.rem(chip + k, 16) * 2 + core, col), device_id_type=MESH)
        return 0

    lax.fori_loop(1, 8, greet_col, 0)
    lax.fori_loop(1, 16, greet_row, 0)

    halfway = pl.ds(pl.multiple_of(core * LANES, LANES), LANES)
    db[chip, :, halfway] = data_ref[...].astype(jnp.bfloat16)
    for h in range(2):
        nb[2 * col + h] = noise_ref[:, h * QW:(h + 1) * QW].astype(jnp.bfloat16)
    pl.semaphore_wait(barrier, 23)

    sends = []

    def send_noise(chunk, to_col):
        copy = pltpu.make_async_remote_copy(
            nb.at[pl.ds(2 * chunk, 2)], nb.at[pl.ds(2 * chunk, 2)],
            n_send.at[len([s for s in sends if s[0] == "n"])], n_recv.at[chunk],
            device_id=(row, to_col), device_id_type=MESH)
        copy.start()
        sends.append(("n", copy))

    def wait_noise(chunk):
        pltpu.make_async_remote_copy(
            nb.at[pl.ds(2 * chunk, 2)], nb.at[pl.ds(2 * chunk, 2)], n_send.at[0], n_recv.at[chunk],
            device_id=(row, col), device_id_type=MESH).wait_recv()

    def send_data(q, to_chip):
        copy = pltpu.make_async_remote_copy(
            db.at[q, :, halfway], db.at[q, :, halfway],
            d_send.at[len([s for s in sends if s[0] == "d"])], d_recv.at[q],
            device_id=(to_chip * 2 + core, col), device_id_type=MESH)
        copy.start()
        sends.append(("d", copy))

    def send_sibling(q):
        copy = pltpu.make_async_remote_copy(
            db.at[q, :, halfway], db.at[q, :, halfway],
            s_send.at[len([s for s in sends if s[0] == "s"])], s_recv.at[q],
            device_id=sibling, device_id_type=MESH)
        copy.start()
        sends.append(("s", copy))

    def wait_data(q):
        pltpu.make_async_remote_copy(
            db.at[q, :, halfway], db.at[q, :, halfway], d_send.at[0], d_recv.at[q],
            device_id=sibling, device_id_type=MESH).wait_recv()

    otherway = pl.ds(pl.multiple_of((1 - core) * LANES, LANES), LANES)

    def wait_sibling(q):
        pltpu.make_async_remote_copy(
            db.at[q, :, otherway], db.at[q, :, otherway], s_send.at[0], s_recv.at[q],
            device_id=sibling, device_id_type=MESH).wait_recv()

    def pass_data(q, forward):
        wait_data(q)
        for shift in forward:
            send_data(q, at_z(shift))
        send_sibling(q)

    send_data(chip, at_z(0, True))
    send_data(chip, at_z(1))
    send_data(chip, at_z(-1))
    send_noise(col, at_x(0, True))
    send_noise(col, at_x(1))
    send_noise(col, at_x(-1))
    send_sibling(chip)

    pass_data(at_z(-1), (1,))
    pass_data(at_z(1), (-1,))
    pass_data(at_z(0, True), (1, -1))
    wait_noise(at_x(-1))
    send_noise(at_x(-1), at_x(1))
    wait_noise(at_x(1))
    wait_noise(at_x(0, True))
    send_noise(at_x(0, True), at_x(1))
    send_noise(at_x(0, True), at_x(-1))
    pass_data(at_z(-1, True), (1,))
    pass_data(at_z(1, True), (-1,))
    pass_data(at_z(-2), (1,))
    pass_data(at_z(2), (-1,))
    pass_data(at_z(-2, True), (1,))
    pass_data(at_z(2, True), (-1,))
    pass_data(at_z(-3), (1,))
    pass_data(at_z(3), ())
    wait_noise(at_x(1, True))
    send_noise(at_x(1, True), at_x(-1))
    wait_noise(at_x(-1, True))
    pass_data(at_z(-3, True), ())
    pass_data(at_z(3, True), (-1,))
    wait_noise(at_x(2))
    wait_noise(at_x(2, True))
    pass_data(at_z(4), ())
    pass_data(at_z(4, True), ())
    for q in range(QS):
        wait_sibling(q)

    scores[...] = jnp.zeros_like(scores)
    sq_n[...] = jnp.zeros_like(sq_n)
    sq_d[...] = jnp.zeros_like(sq_d)

    def block(q, _):
        def strip(t, _):
            at = pl.ds(pl.multiple_of(t * QW, QW), QW)
            scores[:, at] += lax.dot_general(
                nb[q], db[q, at, :], (((1,), (1,)), ((), ())), preferred_element_type=jnp.float32)
            wide = db[q, at, :].astype(jnp.float32)
            wide = wide * wide
            sq_d[at, :] += wide[:, :LANES] + wide[:, LANES:]
            return 0
        lax.fori_loop(0, COLS // QW, strip, 0)

        def norm(t, _):
            at = pl.ds(pl.multiple_of(t * LANES, LANES), LANES)
            wide = nb[q, at, :].astype(jnp.float32)
            wide = wide * wide
            sq_n[at, :] += wide[:, :LANES] + wide[:, LANES:]
            return 0
        lax.fori_loop(0, ROWS // LANES, norm, 0)
        return 0

    lax.fori_loop(0, QS, block, 0)

    scale = LOG2E / (entropic_epsilon * D)

    def norm_row(t, _):
        at = pl.ds(pl.multiple_of(t * LANES, LANES), LANES)
        data_row[:, at] = jnp.sum(sq_d[at, :].T, axis=0, keepdims=True)
        return 0

    lax.fori_loop(0, COLS // LANES, norm_row, 0)
    group = 32

    def score(t, _):
        at = pl.ds(pl.multiple_of(t * group, group), group)
        norms = jnp.sum(sq_n[at, :], axis=1, keepdims=True)
        scores[at, :] = (2.0 * scores[at, :] - norms - data_row[...]) * scale
        return 0

    lax.fori_loop(0, ROWS // group, score, 0)
    data_row[...] = jnp.zeros_like(data_row)

    def noise_step(e):
        def pass_over(t, _):
            at = pl.ds(pl.multiple_of(t * group, group), group)
            terms = [scores[at, c * LANES:(c + 1) * LANES] + data_row[:, c * LANES:(c + 1) * LANES]
                     for c in range(COLS // LANES)]
            largest = terms[0]
            for term in terms[1:]:
                largest = jnp.maximum(largest, term)
            sums = jnp.exp2(terms[0] - largest)
            for term in terms[1:]:
                sums = sums + jnp.exp2(term - largest)
            lane_lse[at, :] = largest + jnp.log(sums) * LOG2E
            return 0
        lax.fori_loop(0, ROWS // group, pass_over, 0)
        for b in range(ROWS // LANES):
            at = slice(b * LANES, (b + 1) * LANES)
            row_x[e, pl.ds(col, 1), :, at] = log2sumexp2(lane_lse[at, :].T)[None]

        def send(k, _):
            pltpu.make_async_remote_copy(
                row_x.at[e, col], row_x.at[e, col], rx_send.at[e, k], rx_recv.at[e, col],
                device_id=(row, lax.rem(col + k, 8)), device_id_type=MESH).start()
            return 0

        def arrive(k, _):
            source = lax.rem(col + k, 8)
            pltpu.make_async_remote_copy(
                row_x.at[e, source], row_x.at[e, source], rx_send.at[e, k], rx_recv.at[e, source],
                device_id=(row, source), device_id_type=MESH).wait()
            return 0

        lax.fori_loop(1, 8, send, 0)
        lax.fori_loop(1, 8, arrive, 0)
        potential = -log2sumexp2(row_x[e])[0] - math.log2(16384)
        for b in range(ROWS // LANES):
            at = slice(b * LANES, (b + 1) * LANES)
            noise_col[at, :] = jnp.broadcast_to(potential[:, at], (LANES, LANES)).T

    def data_step(e):
        def pass_over(t, _):
            at = pl.ds(pl.multiple_of(t * LANES, LANES), LANES)
            partial = []
            for h in range(2):
                rows = slice(h * 256, (h + 1) * 256)
                terms = (scores[rows, at] + noise_col[rows, :]).reshape(32, 8, LANES)
                partial.append(log2sumexp2(terms)[0])
            pair_x[e, 0, :, at] = log2sumexp2(jnp.concatenate(partial, axis=0))
            return 0
        lax.fori_loop(0, COLS // LANES, pass_over, 0)
        swap = pltpu.make_async_remote_copy(
            pair_x.at[e, 0], pair_x.at[e, 1], px_send.at[e], px_recv.at[e],
            device_id=sibling, device_id_type=MESH)
        swap.start()
        swap.wait()
        col_x[e, pl.ds(chip, 1)] = log2sumexp2(pair_x[e])

        def send(k, _):
            pltpu.make_async_remote_copy(
                col_x.at[e, chip], col_x.at[e, chip], cx_send.at[e, k], cx_recv.at[e, chip],
                device_id=(lax.rem(chip + k, 16) * 2 + core, col), device_id_type=MESH).start()
            return 0

        def arrive(k, _):
            source = lax.rem(chip + k, 16)
            pltpu.make_async_remote_copy(
                col_x.at[e, source], col_x.at[e, source], cx_send.at[e, k], cx_recv.at[e, source],
                device_id=(source * 2 + core, col), device_id_type=MESH).wait()
            return 0

        lax.fori_loop(1, 16, send, 0)
        lax.fori_loop(1, 16, arrive, 0)
        data_row[...] = -log2sumexp2(col_x[e])[0] - math.log2(8192)

    for e in range(SWEEPS):
        noise_step(e)
        data_step(e)
    noise_step(SWEEPS)

    def transport(t, _):
        at = pl.ds(pl.multiple_of(t * group, group), group)
        for c in range(COLS // LANES):
            lanes = slice(c * LANES, (c + 1) * LANES)
            plan[at, lanes] = jnp.exp2(noise_col[at, :] + data_row[:, lanes] + scores[at, lanes]).astype(jnp.bfloat16)
        return 0

    lax.fori_loop(0, ROWS // group, transport, 0)

    def spread(k, _):
        target = lax.rem(col + k, 8)
        for h in range(2):
            parts[k, h] = (16384.0 * jnp.dot(
                plan[...], db[2 * target + h], preferred_element_type=jnp.float32)).astype(jnp.bfloat16)
        pltpu.make_async_remote_copy(
            parts.at[k], got.at[k], m_send.at[k], m_recv.at[k],
            device_id=(row, target), device_id_type=MESH).start()
        return 0

    lax.fori_loop(1, 8, spread, 0)
    for h in range(2):
        out_ref[:, h * QW:(h + 1) * QW] = 16384.0 * jnp.dot(
            plan[...], db[2 * col + h], preferred_element_type=jnp.float32)

    def collect(k, _):
        pltpu.make_async_remote_copy(
            parts.at[k], got.at[k], m_send.at[k], m_recv.at[k],
            device_id=(row, lax.rem(col + k, 8)), device_id_type=MESH).wait()
        return 0

    lax.fori_loop(1, 8, collect, 0)

    def total(t, _):
        at = pl.ds(pl.multiple_of(t * group, group), group)
        for h in range(2):
            lanes = slice(h * QW, (h + 1) * QW)
            value = out_ref[at, lanes]
            for k in range(1, 8):
                value = value + got[k, h, at, :].astype(jnp.float32)
            out_ref[at, lanes] = value
        return 0

    lax.fori_loop(0, ROWS // group, total, 0)
    for _, copy in sends:
        copy.wait_send()


def local(noise_latents, data_latents, flow_times):
    bf16, f32 = jnp.bfloat16, jnp.float32
    vmem, dma = pltpu.VMEM, pltpu.SemaphoreType.DMA
    matched = pl.pallas_call(
        kernel,
        out_shape=jax.ShapeDtypeStruct((ROWS, 2 * QW), f32),
        in_specs=[pl.BlockSpec(memory_space=pltpu.VMEM)] * 2,
        out_specs=pl.BlockSpec(memory_space=pltpu.VMEM),
        scratch_shapes=[
            vmem((QS, ROWS, QW), bf16), vmem((QS, COLS, QW), bf16), vmem((ROWS, COLS), f32), vmem((ROWS, COLS), bf16),
            vmem((8, 2, ROWS, QW), bf16), vmem((8, 2, ROWS, QW), bf16),
            vmem((ROWS, LANES), f32), vmem((ROWS, LANES), f32), vmem((1, COLS), f32),
            vmem((ROWS, LANES), f32), vmem((COLS, LANES), f32),
            vmem((SWEEPS + 1, 8, 1, ROWS), f32), vmem((SWEEPS, QS, 1, COLS), f32), vmem((SWEEPS, 2, 1, COLS), f32),
            dma((8,)), dma((8,)), dma((16,)), dma((16,)), dma((16,)), dma((16,)),
            dma((SWEEPS + 1, 8)), dma((SWEEPS + 1, 8)), dma((SWEEPS, 16)), dma((SWEEPS, 16)),
            dma((SWEEPS,)), dma((SWEEPS,)), dma((8,)), dma((8,)),
        ],
        compiler_params=pltpu.CompilerParams(
            collective_id=0, has_side_effects=True, vmem_limit_bytes=48 << 20),
        name="sinkhorn",
    )(noise_latents, data_latents)
    velocity = matched - noise_latents
    interpolant = (1.0 - flow_times)[:, None] * noise_latents + flow_times[:, None] * matched
    return (velocity, interpolant)


def solution(mesh):
    in_specs = (P("row", "col"), P("col", "row"), P("row"))
    out_specs = (P("row", "col"), P("row", "col"))
    return jax.shard_map(local, mesh=mesh, in_specs=in_specs, out_specs=out_specs, check_vma=False)
```

```python
import math

import jax
import jax.numpy as jnp
from jax import lax
from jax.experimental import pallas as pl
from jax.experimental.pallas import tpu as pltpu
from jax.sharding import PartitionSpec as P

D = 4096
SWEEPS = 3
entropic_epsilon = 0.02
MESH = pl.DeviceIdType.MESH
LOG2E = 1.0 / math.log(2.0)

ROWS, COLS = 512, 1024
QS, QW = 16, 256
LANES = 128
X_FIRST = 288
Y_FIRST = ROWS - X_FIRST


def log2sumexp2(values):
    largest = jnp.max(values, axis=0, keepdims=True)
    sums = jnp.sum(jnp.exp2(values - largest), axis=0, keepdims=True)
    return largest + jnp.log(sums) * LOG2E


def kernel(noise_hbm, data_hbm, out_ref,
           noise_ref, data_ref, load_sem,
           nb, db, scores, plan, x_parts, x_got, y_parts, y_got, y_sum, lane_lse, noise_col, weight_col, data_row, sq_n, sq_d,
           row_x, col_x, pair_x,
           n_send, n_recv, d_send, d_recv, s_send, s_recv,
           rx_send, rx_recv, cx_send, cx_recv, px_send, px_recv, m_send, m_recv):
    row, col = lax.axis_index("row"), lax.axis_index("col")
    yhi, z, core = row // 16, lax.rem(row // 2, 8), lax.rem(row, 2)
    x, ylo = col // 2, lax.rem(col, 2)
    chip = row // 2

    def at_x(shift, other=False):
        return lax.rem(x + shift + 4, 4) * 2 + (1 - ylo if other else ylo)

    def at_z(shift, other=False):
        return (1 - yhi if other else yhi) * 8 + lax.rem(z + shift + 8, 8)

    def away(k):
        return lax.rem(4 + jnp.where(lax.rem(k, 2) == 1, (k + 1) // 2, -(k // 2)), 8)

    def row_peer(k):
        other = jnp.where(k < 8, 1 - yhi, yhi)
        return other * 8 + lax.rem(z + away(lax.rem(k, 8)), 8)

    sibling = (row + 1 - 2 * core, col)
    load_noise = pltpu.make_async_copy(noise_hbm, noise_ref, load_sem.at[0])
    load_data = pltpu.make_async_copy(data_hbm, data_ref, load_sem.at[1])
    load_data.start()
    load_noise.start()

    barrier = pltpu.get_barrier_semaphore()
    pl.semaphore_signal(barrier, inc=1, device_id=sibling, device_id_type=MESH)

    def greet_col(k, _):
        pl.semaphore_signal(barrier, inc=1, device_id=(row, lax.rem(col + k, 8)), device_id_type=MESH)
        return 0

    def greet_row(k, _):
        pl.semaphore_signal(barrier, inc=1, device_id=(row_peer(k) * 2 + core, col), device_id_type=MESH)
        return 0

    lax.fori_loop(0, 15, greet_row, 0)
    lax.fori_loop(1, 8, greet_col, 0)

    halfway = pl.ds(pl.multiple_of(core * LANES, LANES), LANES)
    load_data.wait()
    db[chip, :, halfway] = data_ref[...].astype(jnp.bfloat16)
    load_noise.wait()
    for h in range(2):
        nb[2 * col + h] = noise_ref[:, h * QW:(h + 1) * QW].astype(jnp.bfloat16)
    scores[...] = jnp.zeros_like(scores)
    sq_n[...] = jnp.zeros_like(sq_n)
    sq_d[...] = jnp.zeros_like(sq_d)
    pl.semaphore_wait(barrier, 23)

    sends = []

    def send_noise(chunk, to_col):
        copy = pltpu.make_async_remote_copy(
            nb.at[pl.ds(2 * chunk, 2)], nb.at[pl.ds(2 * chunk, 2)],
            n_send.at[len([s for s in sends if s[0] == "n"])], n_recv.at[chunk],
            device_id=(row, to_col), device_id_type=MESH)
        copy.start()
        sends.append(("n", copy))

    def wait_noise(chunk):
        pltpu.make_async_remote_copy(
            nb.at[pl.ds(2 * chunk, 2)], nb.at[pl.ds(2 * chunk, 2)], n_send.at[0], n_recv.at[chunk],
            device_id=(row, col), device_id_type=MESH).wait_recv()

    def send_data(q, to_chip):
        copy = pltpu.make_async_remote_copy(
            db.at[q, :, halfway], db.at[q, :, halfway],
            d_send.at[len([s for s in sends if s[0] == "d"])], d_recv.at[q],
            device_id=(to_chip * 2 + core, col), device_id_type=MESH)
        copy.start()
        sends.append(("d", copy))

    def send_sibling(q):
        copy = pltpu.make_async_remote_copy(
            db.at[q, :, halfway], db.at[q, :, halfway],
            s_send.at[len([s for s in sends if s[0] == "s"])], s_recv.at[q],
            device_id=sibling, device_id_type=MESH)
        copy.start()
        sends.append(("s", copy))

    def wait_data(q):
        pltpu.make_async_remote_copy(
            db.at[q, :, halfway], db.at[q, :, halfway], d_send.at[0], d_recv.at[q],
            device_id=sibling, device_id_type=MESH).wait_recv()

    otherway = pl.ds(pl.multiple_of((1 - core) * LANES, LANES), LANES)

    def wait_sibling(q):
        pltpu.make_async_remote_copy(
            db.at[q, :, otherway], db.at[q, :, otherway], s_send.at[0], s_recv.at[q],
            device_id=sibling, device_id_type=MESH).wait_recv()

    def pass_data(q, forward):
        wait_data(q)
        for shift in forward:
            send_data(q, at_z(shift))
        send_sibling(q)

    def level(c):
        ahead = lax.rem(2 * lax.rem(c, 4) - z + 8, 8)
        after = lax.rem(ahead + 1, 8)
        far = jnp.maximum(jnp.minimum(ahead, 8 - ahead), jnp.minimum(after, 8 - after))
        shift = lax.rem(c // 2 - x + 4, 4)
        late = jnp.logical_and(lax.rem(shift, 2) == 1, lax.rem(c, 2) != ylo)
        return jnp.where(far == 4, 4, jnp.where(shift == 2, 3, jnp.where(jnp.logical_or(far == 3, late), 2, 1)))

    def multiply(now):
        def chunk(c, _):
            @pl.when(level(c) == now)
            def _():
                total = scores[...]
                for h in range(2):
                    total += lax.dot_general(
                        nb[2 * c + h], db[2 * c + h], (((1,), (1,)), ((), ())), preferred_element_type=jnp.float32)
                scores[...] = total

                def data_norm(t, _):
                    at = pl.ds(pl.multiple_of(t * LANES, LANES), LANES)
                    squares = sq_d[at, :]
                    for h in range(2):
                        wide = db[2 * c + h, at, :].astype(jnp.float32)
                        wide = wide * wide
                        squares = squares + (wide[:, :LANES] + wide[:, LANES:])
                    sq_d[at, :] = squares
                    return 0

                def noise_norm(t, _):
                    at = pl.ds(pl.multiple_of(t * LANES, LANES), LANES)
                    squares = sq_n[at, :]
                    for h in range(2):
                        wide = nb[2 * c + h, at, :].astype(jnp.float32)
                        wide = wide * wide
                        squares = squares + (wide[:, :LANES] + wide[:, LANES:])
                    sq_n[at, :] = squares
                    return 0

                lax.fori_loop(0, COLS // LANES, data_norm, 0)
                lax.fori_loop(0, ROWS // LANES, noise_norm, 0)
            return 0
        lax.fori_loop(0, 8, chunk, 0)

    send_data(chip, at_z(0, True))
    send_data(chip, at_z(1))
    send_data(chip, at_z(-1))
    send_noise(col, at_x(0, True))
    send_noise(col, at_x(1))
    send_noise(col, at_x(-1))
    send_sibling(chip)

    pass_data(at_z(-1), (1,))
    pass_data(at_z(1), (-1,))
    pass_data(at_z(0, True), (1, -1))
    wait_noise(at_x(-1))
    send_noise(at_x(-1), at_x(1))
    wait_noise(at_x(1))
    wait_noise(at_x(0, True))
    send_noise(at_x(0, True), at_x(1))
    send_noise(at_x(0, True), at_x(-1))
    pass_data(at_z(-1, True), (1,))
    pass_data(at_z(1, True), (-1,))
    pass_data(at_z(-2), (1,))
    pass_data(at_z(2), (-1,))
    pass_data(at_z(-2, True), (1,))
    pass_data(at_z(2, True), (-1,))
    for shift in (0, 1, -1, 2, -2):
        wait_sibling(at_z(shift))
        wait_sibling(at_z(shift, True))
    multiply(1)
    pass_data(at_z(-3), (1,))
    pass_data(at_z(3), ())
    wait_noise(at_x(1, True))
    send_noise(at_x(1, True), at_x(-1))
    wait_noise(at_x(-1, True))
    pass_data(at_z(-3, True), ())
    pass_data(at_z(3, True), (-1,))
    for shift in (3, -3):
        wait_sibling(at_z(shift))
        wait_sibling(at_z(shift, True))
    multiply(2)
    wait_noise(at_x(2))
    wait_noise(at_x(2, True))
    multiply(3)
    pass_data(at_z(4), ())
    pass_data(at_z(4, True), ())
    wait_sibling(at_z(4))
    wait_sibling(at_z(4, True))
    multiply(4)

    scale = LOG2E / (entropic_epsilon * D)

    def norm_row(t, _):
        at = pl.ds(pl.multiple_of(t * LANES, LANES), LANES)
        data_row[:, at] = jnp.sum(sq_d[at, :].T, axis=0, keepdims=True)
        return 0

    lax.fori_loop(0, COLS // LANES, norm_row, 0)
    group = 32

    def to_column(column_ref, line):
        for b in range(ROWS // LANES):
            at = slice(b * LANES, (b + 1) * LANES)
            column_ref[at, :] = jnp.broadcast_to(line[:, at], (LANES, LANES)).T

    def noise_step(e):
        def pass_over(t, _):
            at = pl.ds(pl.multiple_of(t * group, group), group)
            if e == 0:
                norms = jnp.sum(sq_n[at, :], axis=1, keepdims=True)
                terms = []
                for c in range(COLS // LANES):
                    lanes = slice(c * LANES, (c + 1) * LANES)
                    terms.append((2.0 * scores[at, lanes] - norms - data_row[:, lanes]) * scale)
                    scores[at, lanes] = terms[c]
            else:
                terms = [scores[at, c * LANES:(c + 1) * LANES] + data_row[:, c * LANES:(c + 1) * LANES]
                         for c in range(COLS // LANES)]
            largest = terms[0]
            for term in terms[1:]:
                largest = jnp.maximum(largest, term)
            sums = jnp.exp2(terms[0] - largest)
            for term in terms[1:]:
                sums = sums + jnp.exp2(term - largest)
            lane_lse[at, :] = largest + jnp.log(sums) * LOG2E
            return 0
        lax.fori_loop(0, ROWS // group, pass_over, 0)
        for b in range(ROWS // LANES):
            at = slice(b * LANES, (b + 1) * LANES)
            row_x[e, pl.ds(col, 1), :, at] = log2sumexp2(lane_lse[at, :].T)[None]

        def send(k, _):
            pltpu.make_async_remote_copy(
                row_x.at[e, col], row_x.at[e, col], rx_send.at[e, k], rx_recv.at[e, col],
                device_id=(row, lax.rem(col + k, 8)), device_id_type=MESH).start()
            return 0

        def arrive(k, _):
            source = lax.rem(col + k, 8)
            pltpu.make_async_remote_copy(
                row_x.at[e, source], row_x.at[e, source], rx_send.at[e, k], rx_recv.at[e, source],
                device_id=(row, source), device_id_type=MESH).wait()
            return 0

        lax.fori_loop(1, 8, send, 0)
        return lambda: lax.fori_loop(1, 8, arrive, 0)

    def data_step(e):
        def pass_over(t, _):
            at = pl.ds(pl.multiple_of(t * LANES, LANES), LANES)
            partial = []
            for h in range(2):
                rows = slice(h * 256, (h + 1) * 256)
                terms = (scores[rows, at] + noise_col[rows, :]).reshape(32, 8, LANES)
                partial.append(log2sumexp2(terms)[0])
            pair_x[e, 0, :, at] = log2sumexp2(jnp.concatenate(partial, axis=0))
            return 0
        lax.fori_loop(0, COLS // LANES, pass_over, 0)
        swap = pltpu.make_async_remote_copy(
            pair_x.at[e, 0], pair_x.at[e, 1], px_send.at[e], px_recv.at[e],
            device_id=sibling, device_id_type=MESH)
        swap.start()
        swap.wait()
        col_x[e, pl.ds(chip, 1)] = log2sumexp2(pair_x[e])

        def send(k, _):
            pltpu.make_async_remote_copy(
                col_x.at[e, chip], col_x.at[e, chip], cx_send.at[e, k], cx_recv.at[e, chip],
                device_id=(row_peer(k) * 2 + core, col), device_id_type=MESH).start()
            return 0

        def arrive(k, _):
            source = row_peer(k)
            pltpu.make_async_remote_copy(
                col_x.at[e, source], col_x.at[e, source], cx_send.at[e, k], cx_recv.at[e, source],
                device_id=(source * 2 + core, col), device_id_type=MESH).wait()
            return 0

        lax.fori_loop(0, 15, send, 0)
        lax.fori_loop(0, 15, arrive, 0)
        data_row[...] = -log2sumexp2(col_x[e])[0] - math.log2(8192)

    for e in range(SWEEPS):
        noise_step(e)()
        to_column(noise_col, -log2sumexp2(row_x[e])[0] - math.log2(16384))
        data_step(e)

    last_arrives = noise_step(SWEEPS)
    to_column(noise_col, row_x[SWEEPS, col])

    def transport(t, _):
        at = pl.ds(pl.multiple_of(t * group, group), group)
        for c in range(COLS // LANES):
            lanes = slice(c * LANES, (c + 1) * LANES)
            plan[at, lanes] = jnp.exp2(data_row[:, lanes] + scores[at, lanes] - noise_col[at, :]).astype(jnp.bfloat16)
        return 0

    lax.fori_loop(0, ROWS // group, transport, 0)

    top, low = slice(0, X_FIRST), slice(X_FIRST, ROWS)
    half = Y_FIRST // 2
    SELF, LEFT, RIGHT, MATE = range(4)

    def chunk_sum(rows, target, h):
        return jnp.dot(plan[rows, :], db[2 * target + h], preferred_element_type=jnp.float32)

    def weigh(value, who, rows):
        weight = weight_col[who, rows, :]
        return jnp.concatenate([value[:, :LANES] * weight, value[:, LANES:] * weight], axis=1)

    def for_halves(body):
        def step(h, _):
            body(h)
            return 0
        lax.fori_loop(0, 2, step, 0)

    def fill(ref, slot, rows, target, add=(), weighed=True):
        def one(h):
            value = chunk_sum(rows, target, h)
            if weighed:
                value = weigh(value, SELF, rows)
            for other, other_slot, who in add:
                term = other[other_slot, h].astype(jnp.float32)
                value = value + (term if who is None else weigh(term, who, rows))
            ref[slot, h] = value.astype(jnp.bfloat16)
        for_halves(one)

    def x_copy(slot, to_col):
        return pltpu.make_async_remote_copy(
            x_parts.at[slot], x_got.at[slot], m_send.at[slot], m_recv.at[slot],
            device_id=(row, to_col), device_id_type=MESH)

    def y_copy(slot, to_col):
        return pltpu.make_async_remote_copy(
            y_parts.at[slot], y_got.at[slot], m_send.at[7 + slot], m_recv.at[7 + slot],
            device_id=(row, to_col), device_id_type=MESH)

    def y_half(which, to_col):
        at = pl.ds(which * half, half)
        return pltpu.make_async_remote_copy(
            y_parts.at[4, :, at, :], y_got.at[4, :, at, :], m_send.at[14 + which], m_recv.at[14 + which],
            device_id=(row, to_col), device_id_type=MESH)

    right, left = at_x(1), at_x(-1)
    mate_col = at_x(0, True)
    x_copies = [x_copy(slot, to) for slot, to in enumerate((right, left, right, left, right, left, mate_col))]
    y_copies = {slot: y_copy(slot, to) for slot, to in ((0, mate_col), (1, mate_col), (2, mate_col), (3, mate_col), (5, right), (6, left))}
    y_halves = [y_half(0, right), y_half(1, left)]

    fill(x_parts, 0, top, at_x(2), weighed=False)
    x_copies[0].start()
    fill(x_parts, 1, top, at_x(2, True), weighed=False)
    x_copies[1].start()
    for slot, target in enumerate((at_x(2, True), at_x(1, True), at_x(-1, True), mate_col)):
        fill(y_parts, slot, low, target, weighed=False)
        y_copies[slot].start()

    last_arrives()
    whole = log2sumexp2(row_x[SWEEPS])[0]
    for who, source in enumerate((col, left, right, mate_col)):
        to_column(weight_col.at[who], jnp.exp2(row_x[SWEEPS, source] - whole))

    fill(x_parts, 2, top, at_x(1, True))
    x_copies[2].start()
    y_copies[0].wait_recv()
    fill(y_parts, 4, low, at_x(2), add=[(y_got, 0, MATE)])
    y_halves[0].start()
    y_halves[1].start()
    x_copies[0].wait_recv()
    fill(x_parts, 4, top, right, add=[(x_got, 0, LEFT)])
    x_copies[4].start()
    x_copies[1].wait_recv()
    fill(x_parts, 5, top, at_x(-1, True), add=[(x_got, 1, RIGHT)])
    x_copies[5].start()
    fill(x_parts, 3, top, left)
    x_copies[3].start()

    def add_half(slot, which):
        at = pl.ds(which * half, half)

        def one(h):
            y_parts[slot, h, at, :] = (
                y_sum[h, at, :] + y_got[4, h, at, :].astype(jnp.float32)).astype(jnp.bfloat16)
            rest = pl.ds((1 - which) * half, half)
            y_parts[slot, h, rest, :] = y_sum[h, rest, :].astype(jnp.bfloat16)
        for_halves(one)

    def fill_sum(target, got_slot):
        def one(h):
            y_sum[h] = (weigh(chunk_sum(low, target, h), SELF, low)
                        + weigh(y_got[got_slot, h].astype(jnp.float32), MATE, low))
        for_halves(one)

    y_copies[1].wait_recv()
    fill_sum(right, 1)
    y_halves[0].wait_recv()
    add_half(5, 0)
    y_copies[5].start()
    y_copies[2].wait_recv()
    fill_sum(left, 2)
    y_halves[1].wait_recv()
    add_half(6, 1)
    y_copies[6].start()

    x_copies[2].wait_recv()
    x_copies[5].wait_recv()
    fill(x_parts, 6, top, mate_col, add=[(x_got, 2, None), (x_got, 5, None)])
    x_copies[6].start()

    y_copies[3].wait_recv()
    fill_sum(col, 3)
    for h in range(2):
        lanes = slice(h * QW, (h + 1) * QW)
        out_ref[top, lanes] = weigh(chunk_sum(top, col, h), SELF, top)
    x_copies[3].wait_recv()
    x_copies[4].wait_recv()
    for h in range(2):
        lanes = slice(h * QW, (h + 1) * QW)
        out_ref[top, lanes] += x_got[3, h].astype(jnp.float32) + x_got[4, h].astype(jnp.float32)
    y_copies[5].wait_recv()
    y_copies[6].wait_recv()
    for h in range(2):
        lanes = slice(h * QW, (h + 1) * QW)
        out_ref[low, lanes] = y_sum[h] + (y_got[5, h].astype(jnp.float32) + y_got[6, h].astype(jnp.float32))
    x_copies[6].wait_recv()
    for h in range(2):
        lanes = slice(h * QW, (h + 1) * QW)
        out_ref[top, lanes] += x_got[6, h].astype(jnp.float32)

    for copy in x_copies + list(y_copies.values()) + y_halves:
        copy.wait_send()
    for _, copy in sends:
        copy.wait_send()


def local(noise_latents, data_latents, flow_times):
    bf16, f32 = jnp.bfloat16, jnp.float32
    vmem, dma = pltpu.VMEM, pltpu.SemaphoreType.DMA
    matched = pl.pallas_call(
        kernel,
        out_shape=jax.ShapeDtypeStruct((ROWS, 2 * QW), f32),
        in_specs=[pl.BlockSpec(memory_space=pl.ANY)] * 2,
        out_specs=pl.BlockSpec(memory_space=pltpu.VMEM),
        scratch_shapes=[
            vmem((ROWS, 2 * QW), f32), vmem((COLS, LANES), f32), dma((2,)),
            vmem((QS, ROWS, QW), bf16), vmem((QS, COLS, QW), bf16), vmem((ROWS, COLS), f32), vmem((ROWS, COLS), bf16),
            vmem((7, 2, X_FIRST, QW), bf16), vmem((7, 2, X_FIRST, QW), bf16),
            vmem((7, 2, Y_FIRST, QW), bf16), vmem((7, 2, Y_FIRST, QW), bf16), vmem((2, Y_FIRST, QW), f32),
            vmem((ROWS, LANES), f32), vmem((ROWS, LANES), f32), vmem((4, ROWS, LANES), f32), vmem((1, COLS), f32),
            vmem((ROWS, LANES), f32), vmem((COLS, LANES), f32),
            vmem((SWEEPS + 1, 8, 1, ROWS), f32), vmem((SWEEPS, QS, 1, COLS), f32), vmem((SWEEPS, 2, 1, COLS), f32),
            dma((8,)), dma((8,)), dma((16,)), dma((16,)), dma((16,)), dma((16,)),
            dma((SWEEPS + 1, 8)), dma((SWEEPS + 1, 8)), dma((SWEEPS, 16)), dma((SWEEPS, 16)),
            dma((SWEEPS,)), dma((SWEEPS,)), dma((16,)), dma((16,)),
        ],
        compiler_params=pltpu.CompilerParams(
            collective_id=0, has_side_effects=True, vmem_limit_bytes=48 << 20),
        name="sinkhorn",
    )(noise_latents, data_latents)
    velocity = matched - noise_latents
    interpolant = (1.0 - flow_times)[:, None] * noise_latents + flow_times[:, None] * matched
    return (velocity, interpolant)


def solution(mesh):
    in_specs = (P("row", "col"), P("col", "row"), P("row"))
    out_specs = (P("row", "col"), P("row", "col"))
    return jax.shard_map(local, mesh=mesh, in_specs=in_specs, out_specs=out_specs, check_vma=False)
```

```python
import math

import jax
import jax.numpy as jnp
from jax import lax
from jax.experimental import pallas as pl
from jax.experimental.pallas import tpu as pltpu
from jax.sharding import PartitionSpec as P

D = 4096
SWEEPS = 3
entropic_epsilon = 0.02
MESH = pl.DeviceIdType.MESH
LOG2E = 1.0 / math.log(2.0)

ROWS, COLS = 512, 1024
QS, QW = 16, 256
LANES = 128
X_FIRST = 288
Y_FIRST = ROWS - X_FIRST
SPLIT = 704
PARTS = ((0, SPLIT // 2), (SPLIT // 2, SPLIT // 2), (SPLIT, COLS - SPLIT),
         (SPLIT, (COLS - SPLIT) // 2), ((COLS + SPLIT) // 2, (COLS - SPLIT) // 2))


def log2sumexp2(values):
    largest = jnp.max(values, axis=0, keepdims=True)
    sums = jnp.sum(jnp.exp2(values - largest), axis=0, keepdims=True)
    return largest + jnp.log(sums) * LOG2E


def kernel(noise_hbm, data_hbm, out_ref,
           noise_ref, data_ref, load_sem,
           nb, db, scores, plan, x_parts, x_got, y_parts, y_got, y_sum, lane_lse, noise_col, weight_col, data_row, top_col, sum_col, sq_n, sq_d,
           row_x, col_x, pair_x,
           n_send, n_recv, d_send, d_recv, s_send, s_recv,
           rx_send, rx_recv, cx_send, cx_recv, px_send, px_recv, m_send, m_recv):
    row, col = lax.axis_index("row"), lax.axis_index("col")
    yhi, z, core = row // 16, lax.rem(row // 2, 8), lax.rem(row, 2)
    x, ylo = col // 2, lax.rem(col, 2)
    chip = row // 2

    def at_x(shift, other=False):
        return lax.rem(x + shift + 4, 4) * 2 + (1 - ylo if other else ylo)

    def at_z(shift, other=False):
        return (1 - yhi if other else yhi) * 8 + lax.rem(z + shift + 8, 8)

    def away(k):
        return lax.rem(4 + jnp.where(lax.rem(k, 2) == 1, (k + 1) // 2, -(k // 2)), 8)

    def row_peer(k):
        other = jnp.where(k < 8, 1 - yhi, yhi)
        return other * 8 + lax.rem(z + away(lax.rem(k, 8)), 8)

    sibling = (row + 1 - 2 * core, col)
    load_noise = pltpu.make_async_copy(noise_hbm, noise_ref, load_sem.at[0])
    load_data = pltpu.make_async_copy(data_hbm, data_ref, load_sem.at[1])
    load_data.start()
    load_noise.start()

    up, down, mate_chip = at_z(1), at_z(-1), at_z(0, True)
    right, left, mate_col = at_x(1), at_x(-1), at_x(0, True)
    barrier = pltpu.get_barrier_semaphore()
    for peer in [sibling] + [(row, c) for c in (right, left, mate_col)] + [
            (c * 2 + core, col) for c in (up, down, mate_chip)]:
        pl.semaphore_signal(barrier, inc=1, device_id=peer, device_id_type=MESH)

    halfway = pl.ds(pl.multiple_of(core * LANES, LANES), LANES)
    load_data.wait()
    db[chip, :, halfway] = data_ref[...].astype(jnp.bfloat16)
    load_noise.wait()
    for h in range(2):
        nb[2 * col + h] = noise_ref[:, h * QW:(h + 1) * QW].astype(jnp.bfloat16)
    scores[...] = jnp.zeros_like(scores)
    sq_n[...] = jnp.zeros_like(sq_n)
    sq_d[...] = jnp.zeros_like(sq_d)
    pl.semaphore_wait(barrier, 7)

    sends = []

    def start(kind, copy):
        copy.start()
        sends.append((kind, copy))

    def number(kind):
        return len([s for s in sends if s[0] == kind])

    def noise_copy(chunk, h, send_at, to_col):
        piece = nb.at[2 * chunk + h]
        return pltpu.make_async_remote_copy(
            piece, piece, n_send.at[send_at], n_recv.at[chunk, h], device_id=(row, to_col), device_id_type=MESH)

    def send_noise(chunk, h, *to_cols):
        for to_col in to_cols:
            start("n", noise_copy(chunk, h, number("n"), to_col))

    def wait_noise(chunk, h):
        noise_copy(chunk, h, 0, col).wait_recv()

    def data_copy(q, part, send_at, to_chip):
        first, size = PARTS[part]
        piece = db.at[q, first:first + size, halfway]
        return pltpu.make_async_remote_copy(
            piece, piece, d_send.at[send_at], d_recv.at[q, part],
            device_id=(to_chip * 2 + core, col), device_id_type=MESH)

    def send_data(q, part, *to_chips):
        for to_chip in to_chips:
            start("d", data_copy(q, part, number("d"), to_chip))

    def wait_data(q, part):
        data_copy(q, part, 0, chip).wait_recv()

    def sibling_copy(q, lanes, send_at):
        return pltpu.make_async_remote_copy(
            db.at[q, :, lanes], db.at[q, :, lanes], s_send.at[send_at], s_recv.at[q],
            device_id=sibling, device_id_type=MESH)

    def send_sibling(q):
        start("s", sibling_copy(q, halfway, number("s")))

    otherway = pl.ds(pl.multiple_of((1 - core) * LANES, LANES), LANES)

    def wait_sibling(q):
        sibling_copy(q, otherway, 0).wait_recv()

    def own_rest(shift):
        for q, on, end in ((at_z(-shift), up, 3), (at_z(shift), down, 4)):
            wait_data(q, 2)
            send_data(q, 2 if shift < 3 else end, on)
            send_data(q, 2, mate_chip)

    def own_data(shift):
        for part in (0, 1):
            wait_data(at_z(-shift), part)
            send_data(at_z(-shift), part, up)
            wait_data(at_z(shift), part)
            if shift < 3:
                send_data(at_z(shift), part, down)
        send_sibling(at_z(-shift))
        send_sibling(at_z(shift))

    def mate_data(shift):
        for part in (0, 1):
            wait_data(at_z(-shift, True), part)
            if shift < 3:
                send_data(at_z(-shift, True), part, up)
            wait_data(at_z(shift, True), part)
            send_data(at_z(shift, True), part, down)

    def mate_rest(*shifts):
        for shift in shifts:
            wait_data(at_z(shift, True), 2)
            send_sibling(at_z(shift, True))

    def data_level(q):
        ahead = lax.rem(lax.rem(q, 8) - z + 8, 8)
        far = jnp.minimum(ahead, 8 - ahead)
        own = q // 8 == yhi
        return jnp.where(far == 4, 6, jnp.where(far == 3, jnp.where(own, 4, 5),
                         jnp.where(far == 2, jnp.where(own, 2, 3), jnp.where(jnp.logical_and(own, far == 0), 1, 2))))

    def noise_level(q):
        shift = lax.rem(q // 4 - x + 4, 4)
        mate = lax.rem(q // 2, 2) != ylo
        late = jnp.where(jnp.logical_and(mate, shift >= 2), jnp.where(lax.rem(q, 2) == 0, 4, 6), 3)
        return jnp.where(jnp.logical_or(shift == 2, jnp.logical_and(mate, shift > 0)), late,
                         jnp.where(shift == 0, 1, 2))

    def multiply(now):
        def block(q, _):
            data_at, noise_at = data_level(q), noise_level(q)

            @pl.when(data_at == now)
            def _():
                def strip(t, _):
                    at = pl.ds(pl.multiple_of(t * LANES, LANES), LANES)
                    wide = db[q, at, :].astype(jnp.float32)
                    wide = wide * wide
                    sq_d[at, :] += wide[:, :LANES] + wide[:, LANES:]
                    return 0
                lax.fori_loop(0, COLS // LANES, strip, 0)

            @pl.when(noise_at == now)
            def _():
                def strip(t, _):
                    at = pl.ds(pl.multiple_of(t * LANES, LANES), LANES)
                    wide = nb[q, at, :].astype(jnp.float32)
                    wide = wide * wide
                    sq_n[at, :] += wide[:, :LANES] + wide[:, LANES:]
                    return 0
                lax.fori_loop(0, ROWS // LANES, strip, 0)

            @pl.when(jnp.maximum(noise_at, data_at) == now)
            def _():
                scores[...] += lax.dot_general(
                    nb[q], db[q], (((1,), (1,)), ((), ())), preferred_element_type=jnp.float32)
            return 0

        lax.fori_loop(0, QS, block, 0)

    def arrive(*shifts):
        for shift in shifts:
            wait_sibling(at_z(shift))

    def mate_arrive(*shifts):
        for shift in shifts:
            wait_sibling(at_z(shift, True))

    send_data(chip, 0, mate_chip)
    send_data(chip, 1, mate_chip)
    send_data(chip, 2, up, down)
    for h in (0, 1):
        send_noise(col, h, right, left, mate_col)
    send_data(chip, 0, up, down)
    send_data(chip, 1, up, down)
    send_data(chip, 2, mate_chip)
    send_sibling(chip)

    own_rest(1)
    own_data(1)
    for part in (0, 1):
        wait_data(mate_chip, part)
        send_data(mate_chip, part, up, down)
    wait_noise(left, 0)
    send_noise(left, 0, right)
    wait_noise(right, 0)
    wait_noise(mate_col, 0)
    send_noise(mate_col, 0, left)
    own_rest(2)
    wait_noise(left, 1)
    send_noise(left, 1, right)
    wait_noise(right, 1)
    wait_noise(mate_col, 1)
    send_noise(mate_col, 1, left)
    wait_sibling(chip)
    multiply(1)
    own_data(2)
    mate_data(1)
    send_noise(mate_col, 0, right)
    send_noise(mate_col, 1, right)
    own_rest(3)
    mate_rest(0, -1, 1)
    arrive(1, -1, 2, -2)
    mate_arrive(0, 1, -1)
    multiply(2)
    wait_noise(at_x(1, True), 0)
    send_noise(at_x(1, True), 0, left)
    wait_noise(at_x(2), 0)
    own_data(3)
    mate_data(2)
    wait_noise(at_x(1, True), 1)
    send_noise(at_x(1, True), 1, left)
    wait_noise(at_x(2), 1)
    mate_rest(-2, 2)
    mate_arrive(2, -2)
    multiply(3)
    far, far_mate = at_z(4), at_z(4, True)
    for part in (3, 4):
        wait_data(far, part)
        send_data(far, part, mate_chip)
    wait_noise(at_x(-1, True), 0)
    wait_noise(at_x(2, True), 0)
    arrive(3, -3)
    mate_data(3)
    multiply(4)
    mate_rest(-3, 3)
    mate_arrive(3, -3)
    multiply(5)
    wait_data(far, 0)
    wait_data(far, 1)
    send_sibling(far)
    for part in (3, 4, 0, 1):
        wait_data(far_mate, part)
    send_sibling(far_mate)
    wait_noise(at_x(-1, True), 1)
    wait_noise(at_x(2, True), 1)
    arrive(4)
    mate_arrive(4)
    multiply(6)

    scale = LOG2E / (entropic_epsilon * D)

    def norm_row(t, _):
        at = pl.ds(pl.multiple_of(t * LANES, LANES), LANES)
        data_row[:, at] = jnp.sum(sq_d[at, :].T, axis=0, keepdims=True)
        return 0

    lax.fori_loop(0, COLS // LANES, norm_row, 0)
    group = 32

    def to_column(column_ref, line):
        for b in range(ROWS // LANES):
            at = slice(b * LANES, (b + 1) * LANES)
            column_ref[at, :] = jnp.broadcast_to(line[:, at], (LANES, LANES)).T

    def noise_step(e):
        def pass_over(t, _):
            at = pl.ds(pl.multiple_of(t * group, group), group)
            if e == 0:
                norms = jnp.sum(sq_n[at, :], axis=1, keepdims=True)
                terms = []
                for c in range(COLS // LANES):
                    lanes = slice(c * LANES, (c + 1) * LANES)
                    terms.append((2.0 * scores[at, lanes] - norms - data_row[:, lanes]) * scale)
                    scores[at, lanes] = terms[c]
            else:
                terms = [scores[at, c * LANES:(c + 1) * LANES] + data_row[:, c * LANES:(c + 1) * LANES]
                         for c in range(COLS // LANES)]
            largest = terms[0]
            for term in terms[1:]:
                largest = jnp.maximum(largest, term)
            sums = jnp.exp2(terms[0] - largest)
            for term in terms[1:]:
                sums = sums + jnp.exp2(term - largest)
            lane_lse[at, :] = largest + jnp.log(sums) * LOG2E
            return 0
        lax.fori_loop(0, ROWS // group, pass_over, 0, unroll=2)
        for b in range(ROWS // LANES):
            at = slice(b * LANES, (b + 1) * LANES)
            row_x[e, pl.ds(col, 1), :, at] = log2sumexp2(lane_lse[at, :].T)[None]

        def send(k, _):
            pltpu.make_async_remote_copy(
                row_x.at[e, col], row_x.at[e, col], rx_send.at[e, k], rx_recv.at[e, col],
                device_id=(row, lax.rem(col + k, 8)), device_id_type=MESH).start()
            return 0

        def arrive(k, _):
            source = lax.rem(col + k, 8)
            pltpu.make_async_remote_copy(
                row_x.at[e, source], row_x.at[e, source], rx_send.at[e, k], rx_recv.at[e, source],
                device_id=(row, source), device_id_type=MESH).wait()
            return 0

        lax.fori_loop(1, 8, send, 0)
        return lambda: lax.fori_loop(1, 8, arrive, 0)

    def data_step(e):
        def pass_over(t, _):
            at = pl.ds(pl.multiple_of(t * LANES, LANES), LANES)
            largest, sums = [], []
            for h in range(2):
                rows = slice(h * 256, (h + 1) * 256)
                terms = (scores[rows, at] + noise_col[rows, :]).reshape(32, 8, LANES)
                largest.append(jnp.max(terms, axis=0))
                sums.append(jnp.sum(jnp.exp2(terms - largest[h][None]), axis=0))
            both = jnp.maximum(*largest)
            top_col[:, at] = both
            sum_col[:, at] = sums[0] * jnp.exp2(largest[0] - both) + sums[1] * jnp.exp2(largest[1] - both)
            return 0
        lax.fori_loop(0, COLS // LANES, pass_over, 0, unroll=2)
        tops = top_col[...]
        whole = jnp.max(tops, axis=0, keepdims=True)
        sums = jnp.sum(sum_col[...] * jnp.exp2(tops - whole), axis=0, keepdims=True)
        pair_x[e, 0] = whole + jnp.log(sums) * LOG2E
        swap = pltpu.make_async_remote_copy(
            pair_x.at[e, 0], pair_x.at[e, 1], px_send.at[e], px_recv.at[e],
            device_id=sibling, device_id_type=MESH)
        swap.start()
        swap.wait()
        col_x[e, pl.ds(chip, 1)] = log2sumexp2(pair_x[e])

        def send(k, _):
            pltpu.make_async_remote_copy(
                col_x.at[e, chip], col_x.at[e, chip], cx_send.at[e, k], cx_recv.at[e, chip],
                device_id=(row_peer(k) * 2 + core, col), device_id_type=MESH).start()
            return 0

        def arrive(k, _):
            source = row_peer(k)
            pltpu.make_async_remote_copy(
                col_x.at[e, source], col_x.at[e, source], cx_send.at[e, k], cx_recv.at[e, source],
                device_id=(source * 2 + core, col), device_id_type=MESH).wait()
            return 0

        lax.fori_loop(0, 15, send, 0)
        lax.fori_loop(0, 15, arrive, 0)
        data_row[...] = -log2sumexp2(col_x[e])[0] - math.log2(8192)

    for e in range(SWEEPS):
        noise_step(e)()
        to_column(noise_col, -log2sumexp2(row_x[e])[0] - math.log2(16384))
        data_step(e)

    last_arrives = noise_step(SWEEPS)
    to_column(noise_col, row_x[SWEEPS, col])

    def transport(t, _):
        at = pl.ds(pl.multiple_of(t * group, group), group)
        for c in range(COLS // LANES):
            lanes = slice(c * LANES, (c + 1) * LANES)
            plan[at, lanes] = jnp.exp2(data_row[:, lanes] + scores[at, lanes] - noise_col[at, :]).astype(jnp.bfloat16)
        return 0

    lax.fori_loop(0, ROWS // group, transport, 0)

    top, low = slice(0, X_FIRST), slice(X_FIRST, ROWS)
    half = Y_FIRST // 2
    SELF, LEFT, RIGHT, MATE = range(4)

    def chunk_sum(rows, target, h):
        return jnp.dot(plan[rows, :], db[2 * target + h], preferred_element_type=jnp.float32)

    def weigh(value, who, rows):
        weight = weight_col[who, rows, :]
        return jnp.concatenate([value[:, :LANES] * weight, value[:, LANES:] * weight], axis=1)

    def for_halves(body):
        def step(h, _):
            body(h)
            return 0
        lax.fori_loop(0, 2, step, 0)

    def fill(ref, slot, rows, target, add=(), weighed=True):
        def one(h):
            value = chunk_sum(rows, target, h)
            if weighed:
                value = weigh(value, SELF, rows)
            for other, other_slot, who in add:
                term = other[other_slot, h].astype(jnp.float32)
                value = value + (term if who is None else weigh(term, who, rows))
            ref[slot, h] = value.astype(jnp.bfloat16)
        for_halves(one)

    def x_copy(slot, to_col):
        return pltpu.make_async_remote_copy(
            x_parts.at[slot], x_got.at[slot], m_send.at[slot], m_recv.at[slot],
            device_id=(row, to_col), device_id_type=MESH)

    def y_copy(slot, to_col):
        return pltpu.make_async_remote_copy(
            y_parts.at[slot], y_got.at[slot], m_send.at[7 + slot], m_recv.at[7 + slot],
            device_id=(row, to_col), device_id_type=MESH)

    def y_half(which, to_col):
        at = pl.ds(which * half, half)
        return pltpu.make_async_remote_copy(
            y_parts.at[4, :, at, :], y_got.at[4, :, at, :], m_send.at[14 + which], m_recv.at[14 + which],
            device_id=(row, to_col), device_id_type=MESH)

    x_copies = [x_copy(slot, to) for slot, to in enumerate((right, left, right, left, right, left, mate_col))]
    y_copies = {slot: y_copy(slot, to) for slot, to in ((0, mate_col), (1, mate_col), (2, mate_col), (3, mate_col), (5, right), (6, left))}
    y_halves = [y_half(0, right), y_half(1, left)]

    fill(x_parts, 0, top, at_x(2), weighed=False)
    x_copies[0].start()
    fill(x_parts, 1, top, at_x(2, True), weighed=False)
    x_copies[1].start()
    for slot, target in enumerate((at_x(2, True), at_x(1, True), at_x(-1, True), mate_col)):
        fill(y_parts, slot, low, target, weighed=False)
        y_copies[slot].start()

    last_arrives()
    whole = log2sumexp2(row_x[SWEEPS])[0]
    for who, source in enumerate((col, left, right, mate_col)):
        to_column(weight_col.at[who], jnp.exp2(row_x[SWEEPS, source] - whole))

    fill(x_parts, 2, top, at_x(1, True))
    x_copies[2].start()
    y_copies[0].wait_recv()
    fill(y_parts, 4, low, at_x(2), add=[(y_got, 0, MATE)])
    y_halves[0].start()
    y_halves[1].start()
    x_copies[0].wait_recv()
    fill(x_parts, 4, top, right, add=[(x_got, 0, LEFT)])
    x_copies[4].start()
    x_copies[1].wait_recv()
    fill(x_parts, 5, top, at_x(-1, True), add=[(x_got, 1, RIGHT)])
    x_copies[5].start()
    fill(x_parts, 3, top, left)
    x_copies[3].start()

    def add_half(slot, which):
        at = pl.ds(which * half, half)

        def one(h):
            y_parts[slot, h, at, :] = (
                y_sum[h, at, :] + y_got[4, h, at, :].astype(jnp.float32)).astype(jnp.bfloat16)
            rest = pl.ds((1 - which) * half, half)
            y_parts[slot, h, rest, :] = y_sum[h, rest, :].astype(jnp.bfloat16)
        for_halves(one)

    def fill_sum(target, got_slot):
        def one(h):
            y_sum[h] = (weigh(chunk_sum(low, target, h), SELF, low)
                        + weigh(y_got[got_slot, h].astype(jnp.float32), MATE, low))
        for_halves(one)

    y_copies[1].wait_recv()
    fill_sum(right, 1)
    y_halves[0].wait_recv()
    add_half(5, 0)
    y_copies[5].start()
    y_copies[2].wait_recv()
    fill_sum(left, 2)
    y_halves[1].wait_recv()
    add_half(6, 1)
    y_copies[6].start()

    x_copies[2].wait_recv()
    x_copies[5].wait_recv()
    fill(x_parts, 6, top, mate_col, add=[(x_got, 2, None), (x_got, 5, None)])
    x_copies[6].start()

    y_copies[3].wait_recv()
    fill_sum(col, 3)
    for h in range(2):
        lanes = slice(h * QW, (h + 1) * QW)
        out_ref[top, lanes] = weigh(chunk_sum(top, col, h), SELF, top)
    x_copies[3].wait_recv()
    x_copies[4].wait_recv()
    for h in range(2):
        lanes = slice(h * QW, (h + 1) * QW)
        out_ref[top, lanes] += x_got[3, h].astype(jnp.float32) + x_got[4, h].astype(jnp.float32)
    y_copies[5].wait_recv()
    y_copies[6].wait_recv()
    for h in range(2):
        lanes = slice(h * QW, (h + 1) * QW)
        out_ref[low, lanes] = y_sum[h] + (y_got[5, h].astype(jnp.float32) + y_got[6, h].astype(jnp.float32))
    x_copies[6].wait_recv()
    for h in range(2):
        lanes = slice(h * QW, (h + 1) * QW)
        out_ref[top, lanes] += x_got[6, h].astype(jnp.float32)

    for copy in x_copies + list(y_copies.values()) + y_halves:
        copy.wait_send()
    for _, copy in sends:
        copy.wait_send()


def local(noise_latents, data_latents, flow_times):
    bf16, f32 = jnp.bfloat16, jnp.float32
    vmem, dma = pltpu.VMEM, pltpu.SemaphoreType.DMA
    matched = pl.pallas_call(
        kernel,
        out_shape=jax.ShapeDtypeStruct((ROWS, 2 * QW), f32),
        in_specs=[pl.BlockSpec(memory_space=pltpu.HBM)] * 2,
        out_specs=pl.BlockSpec(memory_space=pltpu.VMEM),
        scratch_shapes=[
            vmem((ROWS, 2 * QW), f32), vmem((COLS, LANES), f32), dma((2,)),
            vmem((QS, ROWS, QW), bf16), vmem((QS, COLS, QW), bf16), vmem((ROWS, COLS), f32), vmem((ROWS, COLS), bf16),
            vmem((7, 2, X_FIRST, QW), bf16), vmem((7, 2, X_FIRST, QW), bf16),
            vmem((7, 2, Y_FIRST, QW), bf16), vmem((7, 2, Y_FIRST, QW), bf16), vmem((2, Y_FIRST, QW), f32),
            vmem((ROWS, LANES), f32), vmem((ROWS, LANES), f32), vmem((4, ROWS, LANES), f32), vmem((1, COLS), f32), vmem((8, COLS), f32), vmem((8, COLS), f32),
            vmem((ROWS, LANES), f32), vmem((COLS, LANES), f32),
            vmem((SWEEPS + 1, 8, 1, ROWS), f32), vmem((SWEEPS, QS, 1, COLS), f32), vmem((SWEEPS, 2, 1, COLS), f32),
            dma((14,)), dma((8, 2)), dma((48,)), dma((16, 5)), dma((16,)), dma((16,)),
            dma((SWEEPS + 1, 8)), dma((SWEEPS + 1, 8)), dma((SWEEPS, 16)), dma((SWEEPS, 16)),
            dma((SWEEPS,)), dma((SWEEPS,)), dma((16,)), dma((16,)),
        ],
        compiler_params=pltpu.CompilerParams(
            collective_id=0, has_side_effects=True, vmem_limit_bytes=60 << 20),
        name="sinkhorn",
    )(noise_latents, data_latents)
    velocity = matched - noise_latents
    interpolant = noise_latents + flow_times[:, None] * velocity
    return (velocity, interpolant)


def solution(mesh):
    in_specs = (P("row", "col"), P("col", "row"), P("row"))
    out_specs = (P("row", "col"), P("row", "col"))
    return jax.shard_map(local, mesh=mesh, in_specs=in_specs, out_specs=out_specs, check_vma=False)
```

```python
import math

import jax
import jax.numpy as jnp
from jax import lax
from jax.experimental import pallas as pl
from jax.experimental.pallas import tpu as pltpu
from jax.sharding import PartitionSpec as P

D = 4096
SWEEPS = 3
entropic_epsilon = 0.02
MESH = pl.DeviceIdType.MESH
LOG2E = 1.0 / math.log(2.0)

ROWS, COLS = 512, 1024
QS, QW = 16, 256
LANES = 128
COL_ORDER = (4, 3, 5, 2, 6, 1, 7)
X_FIRST = 288
Y_FIRST = ROWS - X_FIRST
SPLIT = 640
PARTS = ((0, SPLIT // 2), (SPLIT // 2, SPLIT // 2), (SPLIT, COLS - SPLIT),
         (SPLIT, (COLS - SPLIT) // 2), ((COLS + SPLIT) // 2, (COLS - SPLIT) // 2), (0, COLS))
WHOLE = 5


def log2sumexp2(values):
    largest = jnp.max(values, axis=0, keepdims=True)
    sums = jnp.sum(jnp.exp2(values - largest), axis=0, keepdims=True)
    return largest + jnp.log(sums) * LOG2E


def kernel(noise_hbm, data_hbm, out_ref,
           noise_ref, data_ref, load_sem,
           nb, db, scores, plan, x_parts, x_got, y_parts, y_got, y_sum, lane_lse, noise_col, weight_col, data_row, top_col, sum_col, sq_n, sq_d,
           row_x, col_x, pair_x,
           n_send, n_recv, d_send, d_recv, s_send, s_recv,
           rx_send, rx_recv, cx_send, cx_recv, px_send, px_recv, m_send, m_recv):
    row, col = lax.axis_index("row"), lax.axis_index("col")
    yhi, z, core = row // 16, lax.rem(row // 2, 8), lax.rem(row, 2)
    x, ylo = col // 2, lax.rem(col, 2)
    chip = row // 2

    def at_x(shift, other=False):
        return lax.rem(x + shift + 4, 4) * 2 + (1 - ylo if other else ylo)

    def at_z(shift, other=False):
        return (1 - yhi if other else yhi) * 8 + lax.rem(z + shift + 8, 8)

    def away(k):
        return (4 + (k + 1) // 2 if k % 2 else 4 - k // 2) % 8

    def row_peer(k):
        return (1 - yhi if k < 8 else yhi) * 8 + lax.rem(z + away(k % 8), 8)

    sibling = (row + 1 - 2 * core, col)
    load_noise = pltpu.make_async_copy(noise_hbm, noise_ref, load_sem.at[0])
    load_data = pltpu.make_async_copy(data_hbm, data_ref, load_sem.at[1])
    load_data.start()
    load_noise.start()

    up, down, mate_chip = at_z(1), at_z(-1), at_z(0, True)
    right, left, mate_col = at_x(1), at_x(-1), at_x(0, True)
    barrier = pltpu.get_barrier_semaphore()
    for peer in [sibling] + [(row, c) for c in (right, left, mate_col)] + [
            (c * 2 + core, col) for c in (up, down, mate_chip)]:
        pl.semaphore_signal(barrier, inc=1, device_id=peer, device_id_type=MESH)

    halfway = pl.ds(pl.multiple_of(core * LANES, LANES), LANES)
    load_data.wait()
    db[chip, :, halfway] = data_ref[...].astype(jnp.bfloat16)
    pl.semaphore_wait(barrier, 7)

    sends = []

    def start(kind, copy):
        copy.start()
        sends.append((kind, copy))

    def number(kind):
        return len([s for s in sends if s[0] == kind])

    def noise_copy(chunk, h, send_at, to_col):
        piece = nb.at[2 * chunk + h]
        return pltpu.make_async_remote_copy(
            piece, piece, n_send.at[send_at], n_recv.at[chunk, h], device_id=(row, to_col), device_id_type=MESH)

    def send_noise(chunk, h, *to_cols):
        for to_col in to_cols:
            start("n", noise_copy(chunk, h, number("n"), to_col))

    def wait_noise(chunk, h):
        noise_copy(chunk, h, 0, col).wait_recv()

    def data_copy(q, part, send_at, to_chip):
        first, size = PARTS[part]
        piece = db.at[q, first:first + size, halfway]
        return pltpu.make_async_remote_copy(
            piece, piece, d_send.at[send_at], d_recv.at[q, part],
            device_id=(to_chip * 2 + core, col), device_id_type=MESH)

    def send_data(q, part, *to_chips):
        for to_chip in to_chips:
            start("d", data_copy(q, part, number("d"), to_chip))

    def wait_data(q, part):
        data_copy(q, part, 0, chip).wait_recv()

    def sibling_copy(q, part, lanes, send_at):
        first, size = PARTS[part]
        piece = db.at[q, first:first + size, lanes]
        return pltpu.make_async_remote_copy(
            piece, piece, s_send.at[send_at], s_recv.at[q, part], device_id=sibling, device_id_type=MESH)

    def send_sibling(q, *parts):
        for part in parts or (WHOLE,):
            start("s", sibling_copy(q, part, halfway, number("s")))

    otherway = pl.ds(pl.multiple_of((1 - core) * LANES, LANES), LANES)

    def wait_sibling(q, *parts):
        for part in parts or (WHOLE,):
            sibling_copy(q, part, otherway, 0).wait_recv()

    def own_rest(shift):
        for q, on, end in ((at_z(-shift), up, 3), (at_z(shift), down, 4)):
            wait_data(q, 2)
            send_data(q, 2 if shift < 3 else end, on)
            send_data(q, 2, mate_chip)

    def own_data(shift):
        for part in (0, 1):
            wait_data(at_z(-shift), part)
            send_data(at_z(-shift), part, up)
            wait_data(at_z(shift), part)
            if shift < 3:
                send_data(at_z(shift), part, down)
        send_sibling(at_z(-shift))
        send_sibling(at_z(shift))

    def mate_data(shift):
        for part in (0, 1):
            wait_data(at_z(-shift, True), part)
            if shift < 3:
                send_data(at_z(-shift, True), part, up)
            wait_data(at_z(shift, True), part)
            send_data(at_z(shift, True), part, down)

    def mate_rest(*shifts):
        for shift in shifts:
            wait_data(at_z(shift, True), 2)
            send_sibling(at_z(shift, True))

    def data_level(q):
        ahead = lax.rem(lax.rem(q, 8) - z + 8, 8)
        far = jnp.minimum(ahead, 8 - ahead)
        return jnp.where(q // 8 == yhi, by_shift(far, (1, 2, 5, 7, 9)), by_shift(far, (3, 4, 6, 8, 9)))

    def by_shift(shift, levels):
        level = levels[-1]
        for at, value in enumerate(levels[:-1]):
            level = jnp.where(shift == at, value, level)
        return level

    def noise_level(q):
        shift, late = lax.rem(q // 4 - x + 4, 4), lax.rem(q, 2) == 1
        return jnp.where(lax.rem(q // 2, 2) == ylo, by_shift(shift, (1, 2, jnp.where(late, 6, 5), 2)),
                         by_shift(shift, (3, jnp.where(late, 6, 5), jnp.where(late, 9, 8))))

    def multiply(now):
        def block(q, _):
            @pl.when(jnp.maximum(noise_level(q), data_level(q)) == now)
            def _():
                for t in range(COLS // QW):
                    at, noise_at = slice(t * QW, (t + 1) * QW), slice(t * LANES, (t + 1) * LANES)
                    scores[:, at] += lax.dot_general(
                        nb[q], db[q, at, :], (((1,), (1,)), ((), ())), preferred_element_type=jnp.float32)
                    wide = db[q, at, :].astype(jnp.float32)
                    wide = wide * wide
                    sq_d[at, :] += wide[:, :LANES] + wide[:, LANES:]
                    wide = nb[q, noise_at, :].astype(jnp.float32)
                    wide = wide * wide
                    sq_n[noise_at, :] += wide[:, :LANES] + wide[:, LANES:]
            return 0

        lax.fori_loop(0, QS, block, 0)

    def arrive(*shifts):
        for shift in shifts:
            wait_sibling(at_z(shift))

    def mate_arrive(*shifts):
        for shift in shifts:
            wait_sibling(at_z(shift, True))

    send_data(chip, 0, mate_chip)
    send_data(chip, 1, mate_chip)
    send_data(chip, 2, up, down)
    load_noise.wait()
    for h in (0, 1):
        nb[2 * col + h] = noise_ref[:, h * QW:(h + 1) * QW].astype(jnp.bfloat16)
        send_noise(col, h, right, left, mate_col)
    send_data(chip, 0, up, down)
    send_data(chip, 1, up, down)
    send_data(chip, 2, mate_chip)
    send_sibling(chip)
    scores[...] = jnp.zeros_like(scores)
    sq_n[...] = jnp.zeros_like(sq_n)
    sq_d[...] = jnp.zeros_like(sq_d)

    own_rest(1)
    own_data(1)
    wait_noise(left, 0)
    send_noise(left, 0, right)
    wait_noise(right, 0)
    for part in (0, 1):
        wait_data(mate_chip, part)
        send_data(mate_chip, part, up, down)
    wait_noise(mate_col, 0)
    send_noise(mate_col, 0, left)
    own_rest(2)
    arrive(0)
    multiply(1)
    wait_noise(left, 1)
    send_noise(left, 1, right)
    wait_noise(right, 1)
    own_data(2)
    mate_rest(0)
    arrive(1, -1)
    multiply(2)
    wait_noise(mate_col, 1)
    send_noise(mate_col, 1, left)
    mate_data(1)
    send_noise(mate_col, 0, right)
    send_noise(mate_col, 1, right)
    own_rest(3)
    mate_rest(-1, 1)
    mate_arrive(0)
    multiply(3)
    wait_noise(at_x(1, True), 0)
    send_noise(at_x(1, True), 0, left)
    wait_noise(at_x(2), 0)
    own_data(3)
    mate_arrive(1, -1)
    multiply(4)
    mate_data(2)
    arrive(2, -2)
    multiply(5)
    wait_noise(at_x(1, True), 1)
    send_noise(at_x(1, True), 1, left)
    wait_noise(at_x(2), 1)
    mate_rest(-2, 2)
    far, far_mate = at_z(4), at_z(4, True)
    for part in (3, 4):
        wait_data(far, part)
        send_data(far, part, mate_chip)
    send_sibling(far, 2)
    mate_arrive(2, -2)
    multiply(6)
    arrive(3, -3)
    multiply(7)
    mate_data(3)
    mate_rest(-3, 3)
    wait_noise(at_x(-1, True), 0)
    wait_noise(at_x(2, True), 0)
    mate_arrive(3, -3)
    multiply(8)
    for part in (0, 1):
        wait_data(far, part)
        send_sibling(far, part)
    for part in (3, 4):
        wait_data(far_mate, part)
    send_sibling(far_mate, 2)
    for part in (0, 1):
        wait_data(far_mate, part)
        send_sibling(far_mate, part)
    wait_noise(at_x(-1, True), 1)
    wait_noise(at_x(2, True), 1)
    wait_sibling(far, 2, 0, 1)
    wait_sibling(far_mate, 2, 0, 1)
    multiply(9)

    scale = LOG2E / (entropic_epsilon * D)

    def norm_row(t, _):
        at = pl.ds(pl.multiple_of(t * LANES, LANES), LANES)
        data_row[:, at] = jnp.sum(sq_d[at, :].T, axis=0, keepdims=True)
        return 0

    lax.fori_loop(0, COLS // LANES, norm_row, 0)
    group = 32

    def to_column(column_ref, line):
        for b in range(ROWS // LANES):
            at = slice(b * LANES, (b + 1) * LANES)
            column_ref[at, :] = jnp.broadcast_to(line[:, at], (LANES, LANES)).T

    def noise_step(e):
        def pass_over(t, _):
            at = pl.ds(pl.multiple_of(t * group, group), group)
            if e == 0:
                norms = jnp.sum(sq_n[at, :], axis=1, keepdims=True)
                terms = []
                for c in range(COLS // LANES):
                    lanes = slice(c * LANES, (c + 1) * LANES)
                    terms.append((2.0 * scores[at, lanes] - norms - data_row[:, lanes]) * scale)
                    scores[at, lanes] = terms[c]
            else:
                terms = [scores[at, c * LANES:(c + 1) * LANES] + data_row[:, c * LANES:(c + 1) * LANES]
                         for c in range(COLS // LANES)]
            largest = terms[0]
            for term in terms[1:]:
                largest = jnp.maximum(largest, term)
            sums = jnp.exp2(terms[0] - largest)
            for term in terms[1:]:
                sums = sums + jnp.exp2(term - largest)
            lane_lse[at, :] = largest + jnp.log(sums) * LOG2E
            return 0
        lax.fori_loop(0, ROWS // group, pass_over, 0, unroll=2)
        for b in range(ROWS // LANES):
            at = slice(b * LANES, (b + 1) * LANES)
            row_x[e, pl.ds(col, 1), :, at] = log2sumexp2(lane_lse[at, :].T)[None]

        for k in COL_ORDER:
            row_copy(e, col, k).start()

    def row_copy(e, source, k):
        return pltpu.make_async_remote_copy(
            row_x.at[e, source], row_x.at[e, source], rx_send.at[e, k], rx_recv.at[e, source],
            device_id=(row, lax.rem(col + k, 8)), device_id_type=MESH)

    def noise_arrives(e):
        for k in COL_ORDER[::-1]:
            row_copy(e, lax.rem(col + k, 8), k).wait_recv()

    def col_copy(e, source, k):
        return pltpu.make_async_remote_copy(
            col_x.at[e, source], col_x.at[e, source], cx_send.at[e, k], cx_recv.at[e, source],
            device_id=(row_peer(k) * 2 + core, col), device_id_type=MESH)

    def swap_copy(e):
        return pltpu.make_async_remote_copy(
            pair_x.at[e, 0], pair_x.at[e, 1], px_send.at[e], px_recv.at[e],
            device_id=sibling, device_id_type=MESH)

    def data_step(e):
        def pass_over(t, _):
            at = pl.ds(pl.multiple_of(t * LANES, LANES), LANES)
            largest, sums = [], []
            for h in range(2):
                rows = slice(h * 256, (h + 1) * 256)
                terms = (scores[rows, at] + noise_col[rows, :]).reshape(32, 8, LANES)
                largest.append(jnp.max(terms, axis=0))
                sums.append(jnp.sum(jnp.exp2(terms - largest[h][None]), axis=0))
            both = jnp.maximum(*largest)
            top_col[:, at] = both
            sum_col[:, at] = sums[0] * jnp.exp2(largest[0] - both) + sums[1] * jnp.exp2(largest[1] - both)
            return 0
        lax.fori_loop(0, COLS // LANES, pass_over, 0, unroll=2)
        tops = top_col[...]
        whole = jnp.max(tops, axis=0, keepdims=True)
        sums = jnp.sum(sum_col[...] * jnp.exp2(tops - whole), axis=0, keepdims=True)
        pair_x[e, 0] = whole + jnp.log(sums) * LOG2E
        swap = swap_copy(e)
        swap.start()
        swap.wait_recv()
        col_x[e, pl.ds(chip, 1)] = log2sumexp2(pair_x[e])

        for k in range(15):
            col_copy(e, chip, k).start()
        for k in range(14, -1, -1):
            col_copy(e, row_peer(k), k).wait_recv()
        data_row[...] = -log2sumexp2(col_x[e])[0] - math.log2(8192)

    for e in range(SWEEPS):
        noise_step(e)
        noise_arrives(e)
        to_column(noise_col, -log2sumexp2(row_x[e])[0] - math.log2(16384))
        data_step(e)

    noise_step(SWEEPS)
    to_column(noise_col, row_x[SWEEPS, col])

    def transport(t, _):
        at = pl.ds(pl.multiple_of(t * group, group), group)
        for c in range(COLS // LANES):
            lanes = slice(c * LANES, (c + 1) * LANES)
            plan[at, lanes] = jnp.exp2(data_row[:, lanes] + scores[at, lanes] - noise_col[at, :]).astype(jnp.bfloat16)
        return 0

    lax.fori_loop(0, ROWS // group, transport, 0)

    top, low = slice(0, X_FIRST), slice(X_FIRST, ROWS)
    half = Y_FIRST // 2
    SELF, LEFT, RIGHT, MATE = range(4)

    def chunk_sum(rows, target, h):
        return jnp.dot(plan[rows, :], db[2 * target + h], preferred_element_type=jnp.float32)

    def weigh(value, who, rows):
        weight = weight_col[who, rows, :]
        return jnp.concatenate([value[:, :LANES] * weight, value[:, LANES:] * weight], axis=1)

    def fill(ref, slot, h, rows, target, add=(), weighed=True):
        value = chunk_sum(rows, target, h)
        if weighed:
            value = weigh(value, SELF, rows)
        for other, other_slot, who in add:
            term = other[other_slot, h].astype(jnp.float32)
            value = value + (term if who is None else weigh(term, who, rows))
        ref[slot, h] = value.astype(jnp.bfloat16)

    def x_copy(slot, h, to_col):
        return pltpu.make_async_remote_copy(
            x_parts.at[slot, h], x_got.at[slot, h], m_send.at[slot, h], m_recv.at[slot, h],
            device_id=(row, to_col), device_id_type=MESH)

    def y_copy(slot, h, to_col):
        return pltpu.make_async_remote_copy(
            y_parts.at[slot, h], y_got.at[slot, h], m_send.at[7 + slot, h], m_recv.at[7 + slot, h],
            device_id=(row, to_col), device_id_type=MESH)

    def y_half(which, h, to_col):
        at = pl.ds(which * half, half)
        return pltpu.make_async_remote_copy(
            y_parts.at[4, h, at, :], y_got.at[4, h, at, :], m_send.at[14 + which, h], m_recv.at[14 + which, h],
            device_id=(row, to_col), device_id_type=MESH)

    x_copies = [[x_copy(slot, h, to) for h in range(2)]
                for slot, to in enumerate((right, left, right, left, right, left, mate_col))]
    y_copies = {slot: [y_copy(slot, h, to) for h in range(2)]
                for slot, to in ((0, mate_col), (1, mate_col), (2, mate_col), (3, mate_col), (5, right), (6, left))}
    y_halves = [[y_half(which, h, to) for h in range(2)] for which, to in enumerate((right, left))]

    for h in range(2):
        fill(x_parts, 0, h, top, at_x(2), weighed=False)
        x_copies[0][h].start()
        fill(x_parts, 1, h, top, at_x(2, True), weighed=False)
        x_copies[1][h].start()
        fill(y_parts, 0, h, low, at_x(2, True), weighed=False)
        y_copies[0][h].start()
    for slot, target in ((1, at_x(1, True)), (2, at_x(-1, True)), (3, mate_col)):
        for h in range(2):
            fill(y_parts, slot, h, low, target, weighed=False)
            y_copies[slot][h].start()

    noise_arrives(SWEEPS)
    whole = log2sumexp2(row_x[SWEEPS])[0]
    for who, source in enumerate((col, left, right, mate_col)):
        to_column(weight_col.at[who], jnp.exp2(row_x[SWEEPS, source] - whole))

    for h in range(2):
        y_copies[0][h].wait_recv()
        fill(y_parts, 4, h, low, at_x(2), add=[(y_got, 0, MATE)])
        y_halves[0][h].start()
        y_halves[1][h].start()
        x_copies[1][h].wait_recv()
        fill(x_parts, 5, h, top, at_x(-1, True), add=[(x_got, 1, RIGHT)])
        x_copies[5][h].start()
        fill(x_parts, 2, h, top, at_x(1, True))
        x_copies[2][h].start()
    for h in range(2):
        x_copies[0][h].wait_recv()
        fill(x_parts, 4, h, top, right, add=[(x_got, 0, LEFT)])
        x_copies[4][h].start()
        fill(x_parts, 3, h, top, left)
        x_copies[3][h].start()

    def low_sum(target, h, got_slot):
        return (weigh(chunk_sum(low, target, h), SELF, low)
                + weigh(y_got[got_slot, h].astype(jnp.float32), MATE, low))

    for slot, target, got_slot, which in ((5, right, 1, 0), (6, left, 2, 1)):
        at, rest = pl.ds(which * half, half), pl.ds((1 - which) * half, half)
        for h in range(2):
            y_copies[got_slot][h].wait_recv()
            y_sum[...] = low_sum(target, h, got_slot)
            y_parts[slot, h, rest, :] = y_sum[rest, :].astype(jnp.bfloat16)
            y_halves[which][h].wait_recv()
            y_parts[slot, h, at, :] = (y_sum[at, :] + y_got[4, h, at, :].astype(jnp.float32)).astype(jnp.bfloat16)
            y_copies[slot][h].start()

    for h in range(2):
        x_copies[2][h].wait_recv()
        x_copies[5][h].wait_recv()
        fill(x_parts, 6, h, top, mate_col, add=[(x_got, 2, None), (x_got, 5, None)])
        x_copies[6][h].start()
    for h in range(2):
        lanes = slice(h * QW, (h + 1) * QW)
        y_copies[3][h].wait_recv()
        out_ref[low, lanes] = low_sum(col, h, 3)
        out_ref[top, lanes] = weigh(chunk_sum(top, col, h), SELF, top)
    for h in range(2):
        lanes = slice(h * QW, (h + 1) * QW)
        x_copies[3][h].wait_recv()
        x_copies[4][h].wait_recv()
        out_ref[top, lanes] += x_got[3, h].astype(jnp.float32) + x_got[4, h].astype(jnp.float32)
    for h in range(2):
        lanes = slice(h * QW, (h + 1) * QW)
        y_copies[5][h].wait_recv()
        y_copies[6][h].wait_recv()
        out_ref[low, lanes] += y_got[5, h].astype(jnp.float32) + y_got[6, h].astype(jnp.float32)
        x_copies[6][h].wait_recv()
        out_ref[top, lanes] += x_got[6, h].astype(jnp.float32)

    for pair in x_copies + list(y_copies.values()) + y_halves:
        for copy in pair:
            copy.wait_send()
    for e in range(SWEEPS + 1):
        for k in range(1, 8):
            row_copy(e, col, k).wait_send()
    for e in range(SWEEPS):
        for k in range(15):
            col_copy(e, chip, k).wait_send()
        swap_copy(e).wait_send()
    for _, copy in sends:
        copy.wait_send()


def local(noise_latents, data_latents, flow_times):
    bf16, f32 = jnp.bfloat16, jnp.float32
    vmem, dma = pltpu.VMEM, pltpu.SemaphoreType.DMA
    matched = pl.pallas_call(
        kernel,
        out_shape=jax.ShapeDtypeStruct((ROWS, 2 * QW), f32),
        in_specs=[pl.BlockSpec(memory_space=pltpu.HBM)] * 2,
        out_specs=pl.BlockSpec(memory_space=pltpu.VMEM),
        scratch_shapes=[
            vmem((ROWS, 2 * QW), f32), vmem((COLS, LANES), f32), dma((2,)),
            vmem((QS, ROWS, QW), bf16), vmem((QS, COLS, QW), bf16), vmem((ROWS, COLS), f32), vmem((ROWS, COLS), bf16),
            vmem((7, 2, X_FIRST, QW), bf16), vmem((7, 2, X_FIRST, QW), bf16),
            vmem((7, 2, Y_FIRST, QW), bf16), vmem((7, 2, Y_FIRST, QW), bf16), vmem((Y_FIRST, QW), f32),
            vmem((ROWS, LANES), f32), vmem((ROWS, LANES), f32), vmem((4, ROWS, LANES), f32), vmem((1, COLS), f32), vmem((8, COLS), f32), vmem((8, COLS), f32),
            vmem((ROWS, LANES), f32), vmem((COLS, LANES), f32),
            vmem((SWEEPS + 1, 8, 1, ROWS), f32), vmem((SWEEPS, QS, 1, COLS), f32), vmem((SWEEPS, 2, 1, COLS), f32),
            dma((14,)), dma((8, 2)), dma((48,)), dma((16, 5)), dma((20,)), dma((16, 6)),
            dma((SWEEPS + 1, 8)), dma((SWEEPS + 1, 8)), dma((SWEEPS, 16)), dma((SWEEPS, 16)),
            dma((SWEEPS,)), dma((SWEEPS,)), dma((16, 2)), dma((16, 2)),
        ],
        compiler_params=pltpu.CompilerParams(
            collective_id=0, has_side_effects=True, vmem_limit_bytes=60 << 20),
        name="sinkhorn",
    )(noise_latents, data_latents)
    velocity = matched - noise_latents
    interpolant = noise_latents + flow_times[:, None] * velocity
    return (velocity, interpolant)


def solution(mesh):
    in_specs = (P("row", "col"), P("col", "row"), P("row"))
    out_specs = (P("row", "col"), P("row", "col"))
    return jax.shard_map(local, mesh=mesh, in_specs=in_specs, out_specs=out_specs, check_vma=False)
```

```python
import math

import jax
import jax.numpy as jnp
from jax import lax
from jax.experimental import pallas as pl
from jax.experimental.pallas import tpu as pltpu
from jax.sharding import PartitionSpec as P

D = 4096
SWEEPS = 3
entropic_epsilon = 0.02
MESH = pl.DeviceIdType.MESH
LOG2E = 1.0 / math.log(2.0)

ROWS, COLS = 512, 1024
QS, QW = 16, 256
LANES = 128
COL_ORDER = (4, 3, 5, 2, 6, 1, 7)
X_FIRST = 288
Y_FIRST = ROWS - X_FIRST
SPLIT = 640
PARTS = ((0, SPLIT // 2), (SPLIT // 2, SPLIT // 2), (SPLIT, COLS - SPLIT),
         (SPLIT, (COLS - SPLIT) // 2), ((COLS + SPLIT) // 2, (COLS - SPLIT) // 2), (0, COLS))
WHOLE = 5


def log2sumexp2(values):
    largest = jnp.max(values, axis=0, keepdims=True)
    sums = jnp.sum(jnp.exp2(values - largest), axis=0, keepdims=True)
    return largest + jnp.log(sums) * LOG2E


def kernel(noise_hbm, data_hbm, out_ref,
           noise_ref, data_ref, load_sem,
           nb, db, scores, plan, x_parts, x_got, y_parts, y_got, y_sum, top_row, sum_row, noise_col, weight_col, data_row, top_col, sum_col, sq_n, sq_d,
           row_x, col_x, pair_x,
           n_send, n_recv, d_send, d_recv, s_send, s_recv,
           rx_send, rx_recv, cx_send, cx_recv, px_send, px_recv, m_send, m_recv):
    row, col = lax.axis_index("row"), lax.axis_index("col")
    yhi, z, core = row // 16, lax.rem(row // 2, 8), lax.rem(row, 2)
    x, ylo = col // 2, lax.rem(col, 2)
    chip = row // 2

    def at_x(shift, other=False):
        return lax.rem(x + shift + 4, 4) * 2 + (1 - ylo if other else ylo)

    def at_z(shift, other=False):
        return (1 - yhi if other else yhi) * 8 + lax.rem(z + shift + 8, 8)

    def away(k):
        return (4 + (k + 1) // 2 if k % 2 else 4 - k // 2) % 8

    def row_peer(k):
        return (1 - yhi if k < 8 else yhi) * 8 + lax.rem(z + away(k % 8), 8)

    sibling = (row + 1 - 2 * core, col)
    load_noise = pltpu.make_async_copy(noise_hbm, noise_ref, load_sem.at[0])
    load_data = pltpu.make_async_copy(data_hbm, data_ref, load_sem.at[1])
    load_data.start()
    load_noise.start()

    up, down, mate_chip = at_z(1), at_z(-1), at_z(0, True)
    right, left, mate_col = at_x(1), at_x(-1), at_x(0, True)
    barrier = pltpu.get_barrier_semaphore()
    for peer in [sibling] + [(row, c) for c in (right, left, mate_col)] + [
            (c * 2 + core, col) for c in (up, down, mate_chip)]:
        pl.semaphore_signal(barrier, inc=1, device_id=peer, device_id_type=MESH)

    halfway = pl.ds(pl.multiple_of(core * LANES, LANES), LANES)
    load_data.wait()
    db[chip, :, halfway] = data_ref[...].astype(jnp.bfloat16)
    pl.semaphore_wait(barrier, 7)

    sends = []

    def start(kind, copy):
        copy.start()
        sends.append((kind, copy))

    def number(kind):
        return len([s for s in sends if s[0] == kind])

    def noise_copy(chunk, h, send_at, to_col):
        piece = nb.at[2 * chunk + h]
        return pltpu.make_async_remote_copy(
            piece, piece, n_send.at[send_at], n_recv.at[chunk, h], device_id=(row, to_col), device_id_type=MESH)

    def send_noise(chunk, h, *to_cols):
        for to_col in to_cols:
            start("n", noise_copy(chunk, h, number("n"), to_col))

    def wait_noise(chunk, h):
        noise_copy(chunk, h, 0, col).wait_recv()

    def data_copy(q, part, send_at, to_chip):
        first, size = PARTS[part]
        piece = db.at[q, first:first + size, halfway]
        return pltpu.make_async_remote_copy(
            piece, piece, d_send.at[send_at], d_recv.at[q, part],
            device_id=(to_chip * 2 + core, col), device_id_type=MESH)

    def send_data(q, part, *to_chips):
        for to_chip in to_chips:
            start("d", data_copy(q, part, number("d"), to_chip))

    def wait_data(q, part):
        data_copy(q, part, 0, chip).wait_recv()

    def sibling_copy(q, part, lanes, send_at):
        first, size = PARTS[part]
        piece = db.at[q, first:first + size, lanes]
        return pltpu.make_async_remote_copy(
            piece, piece, s_send.at[send_at], s_recv.at[q, part], device_id=sibling, device_id_type=MESH)

    def send_sibling(q, *parts):
        for part in parts or (WHOLE,):
            start("s", sibling_copy(q, part, halfway, number("s")))

    otherway = pl.ds(pl.multiple_of((1 - core) * LANES, LANES), LANES)

    def wait_sibling(q, *parts):
        for part in parts or (WHOLE,):
            sibling_copy(q, part, otherway, 0).wait_recv()

    def own_rest(shift):
        for q, on, end in ((at_z(-shift), up, 3), (at_z(shift), down, 4)):
            wait_data(q, 2)
            send_data(q, 2 if shift < 3 else end, on)
            send_data(q, 2, mate_chip)

    def own_data(shift):
        for part in (0, 1):
            wait_data(at_z(-shift), part)
            if shift < 3 or part == 0:
                send_data(at_z(-shift), part, up)
            wait_data(at_z(shift), part)
            if shift < 3 or part == 1:
                send_data(at_z(shift), part, down)
        send_sibling(at_z(-shift))
        send_sibling(at_z(shift))

    def mate_data(shift):
        for part in (0, 1):
            wait_data(at_z(-shift, True), part)
            if shift < 3 or part == 0:
                send_data(at_z(-shift, True), part, up)
            wait_data(at_z(shift, True), part)
            if shift < 3 or part == 1:
                send_data(at_z(shift, True), part, down)

    def mate_rest(*shifts):
        for shift in shifts:
            wait_data(at_z(shift, True), 2)
            send_sibling(at_z(shift, True))

    def data_level(q):
        ahead = lax.rem(lax.rem(q, 8) - z + 8, 8)
        far = jnp.minimum(ahead, 8 - ahead)
        return jnp.where(q // 8 == yhi, by_shift(far, (1, 2, 5, 7, 10)), by_shift(far, (3, 4, 6, 8, 10)))

    def by_shift(shift, levels):
        level = levels[-1]
        for at, value in enumerate(levels[:-1]):
            level = jnp.where(shift == at, value, level)
        return level

    def noise_level(q):
        shift, late = lax.rem(q // 4 - x + 4, 4), lax.rem(q, 2) == 1
        return jnp.where(lax.rem(q // 2, 2) == ylo, by_shift(shift, (1, 2, jnp.where(late, 6, 5), 2)),
                         by_shift(shift, (3, jnp.where(late, 6, 5), jnp.where(late, 9, 8))))

    def multiply(now):
        def block(q, _):
            @pl.when(jnp.maximum(noise_level(q), data_level(q)) == now)
            def _():
                for t in range(COLS // QW):
                    at, noise_at = slice(t * QW, (t + 1) * QW), slice(t * LANES, (t + 1) * LANES)
                    scores[:, at] += lax.dot_general(
                        nb[q], db[q, at, :], (((1,), (1,)), ((), ())), preferred_element_type=jnp.float32)
                    wide = db[q, at, :].astype(jnp.float32)
                    wide = wide * wide
                    sq_d[at, :] += wide[:, :LANES] + wide[:, LANES:]
                    wide = nb[q, noise_at, :].astype(jnp.float32)
                    wide = wide * wide
                    sq_n[noise_at, :] += wide[:, :LANES] + wide[:, LANES:]
            return 0

        lax.fori_loop(0, QS, block, 0)

    def arrive(*shifts):
        for shift in shifts:
            wait_sibling(at_z(shift))

    def mate_arrive(*shifts):
        for shift in shifts:
            wait_sibling(at_z(shift, True))

    send_data(chip, 0, mate_chip)
    send_data(chip, 1, mate_chip)
    send_data(chip, 2, up, down)
    load_noise.wait()
    for h in (0, 1):
        nb[2 * col + h] = noise_ref[:, h * QW:(h + 1) * QW].astype(jnp.bfloat16)
        send_noise(col, h, right, left, mate_col)
    send_data(chip, 0, up, down)
    send_data(chip, 1, up, down)
    send_data(chip, 2, mate_chip)
    send_sibling(chip)
    scores[...] = jnp.zeros_like(scores)
    sq_n[...] = jnp.zeros_like(sq_n)
    sq_d[...] = jnp.zeros_like(sq_d)

    own_rest(1)
    own_data(1)
    wait_noise(left, 0)
    send_noise(left, 0, right)
    wait_noise(right, 0)
    for part in (0, 1):
        wait_data(mate_chip, part)
        send_data(mate_chip, part, up, down)
    wait_noise(mate_col, 0)
    send_noise(mate_col, 0, left)
    own_rest(2)
    arrive(0)
    multiply(1)
    wait_noise(left, 1)
    send_noise(left, 1, right)
    wait_noise(right, 1)
    own_data(2)
    mate_rest(0)
    arrive(1, -1)
    multiply(2)
    wait_noise(mate_col, 1)
    send_noise(mate_col, 1, left)
    mate_data(1)
    send_noise(mate_col, 0, right)
    send_noise(mate_col, 1, right)
    own_rest(3)
    mate_rest(-1, 1)
    mate_arrive(0)
    multiply(3)
    wait_noise(at_x(1, True), 0)
    send_noise(at_x(1, True), 0, left)
    wait_noise(at_x(2), 0)
    own_data(3)
    mate_arrive(1, -1)
    multiply(4)
    mate_data(2)
    arrive(2, -2)
    multiply(5)
    wait_noise(at_x(1, True), 1)
    send_noise(at_x(1, True), 1, left)
    wait_noise(at_x(2), 1)
    mate_rest(-2, 2)
    far, far_mate = at_z(4), at_z(4, True)
    for part in (3, 4):
        wait_data(far, part)
        send_data(far, part, mate_chip)
    send_sibling(far, 2)
    mate_arrive(2, -2)
    multiply(6)
    arrive(3, -3)
    mate_data(3)
    multiply(7)
    mate_rest(-3, 3)
    wait_noise(at_x(-1, True), 0)
    wait_noise(at_x(2, True), 0)
    mate_arrive(3, -3)
    multiply(8)
    for part in (0, 1):
        wait_data(far, part)
        send_sibling(far, part)
    for part in (3, 4):
        wait_data(far_mate, part)
    send_sibling(far_mate, 2)
    for part in (0, 1):
        wait_data(far_mate, part)
        send_sibling(far_mate, part)
    wait_noise(at_x(-1, True), 1)
    wait_noise(at_x(2, True), 1)
    multiply(9)
    wait_sibling(far, 2, 0, 1)
    wait_sibling(far_mate, 2, 0, 1)
    multiply(10)

    scale = LOG2E / (entropic_epsilon * D)

    def norm_row(t, _):
        at = pl.ds(pl.multiple_of(t * LANES, LANES), LANES)
        data_row[:, at] = jnp.sum(sq_d[at, :].T, axis=0, keepdims=True)
        return 0

    lax.fori_loop(0, COLS // LANES, norm_row, 0)
    group = 32

    def to_column(column_ref, line):
        for b in range(ROWS // LANES):
            at = slice(b * LANES, (b + 1) * LANES)
            column_ref[at, :] = jnp.broadcast_to(line[:, at], (LANES, LANES)).T

    def noise_step(e):
        def pass_over(t, _):
            at = pl.ds(pl.multiple_of(t * group, group), group)
            if e == 0:
                norms = jnp.sum(sq_n[at, :], axis=1, keepdims=True)
                terms = []
                for c in range(COLS // LANES):
                    lanes = slice(c * LANES, (c + 1) * LANES)
                    terms.append((2.0 * scores[at, lanes] - norms - data_row[:, lanes]) * scale)
                    scores[at, lanes] = terms[c]
            else:
                terms = [scores[at, c * LANES:(c + 1) * LANES] + data_row[:, c * LANES:(c + 1) * LANES]
                         for c in range(COLS // LANES)]
            largest = terms[0]
            for term in terms[1:]:
                largest = jnp.maximum(largest, term)
            sums = jnp.exp2(terms[0] - largest)
            for term in terms[1:]:
                sums = sums + jnp.exp2(term - largest)
            top_row[at, :] = largest
            sum_row[at, :] = sums
            return 0
        lax.fori_loop(0, ROWS // group, pass_over, 0, unroll=4)
        for b in range(ROWS // LANES):
            at = slice(b * LANES, (b + 1) * LANES)
            tops = top_row[at, :].T
            whole = jnp.max(tops, axis=0, keepdims=True)
            sums = jnp.sum(sum_row[at, :].T * jnp.exp2(tops - whole), axis=0, keepdims=True)
            row_x[e, pl.ds(col, 1), :, at] = (whole + jnp.log(sums) * LOG2E)[None]

        for k in COL_ORDER:
            row_copy(e, col, k).start()

    def row_copy(e, source, k):
        return pltpu.make_async_remote_copy(
            row_x.at[e, source], row_x.at[e, source], rx_send.at[e, k], rx_recv.at[e, source],
            device_id=(row, lax.rem(col + k, 8)), device_id_type=MESH)

    def noise_arrives(e):
        for k in COL_ORDER[::-1]:
            row_copy(e, lax.rem(col + k, 8), k).wait_recv()

    def col_copy(e, source, k):
        return pltpu.make_async_remote_copy(
            col_x.at[e, source], col_x.at[e, source], cx_send.at[e, k], cx_recv.at[e, source],
            device_id=(row_peer(k) * 2 + core, col), device_id_type=MESH)

    def swap_copy(e):
        return pltpu.make_async_remote_copy(
            pair_x.at[e, 0], pair_x.at[e, 1], px_send.at[e], px_recv.at[e],
            device_id=sibling, device_id_type=MESH)

    def data_step(e):
        def pass_over(t, _):
            at = pl.ds(pl.multiple_of(t * LANES, LANES), LANES)
            largest, sums = [], []
            for h in range(2):
                rows = slice(h * 256, (h + 1) * 256)
                terms = (scores[rows, at] + noise_col[rows, :]).reshape(32, 8, LANES)
                largest.append(jnp.max(terms, axis=0))
                sums.append(jnp.sum(jnp.exp2(terms - largest[h][None]), axis=0))
            both = jnp.maximum(*largest)
            top_col[:, at] = both
            sum_col[:, at] = sums[0] * jnp.exp2(largest[0] - both) + sums[1] * jnp.exp2(largest[1] - both)
            return 0
        lax.fori_loop(0, COLS // LANES, pass_over, 0, unroll=4)
        tops = top_col[...]
        whole = jnp.max(tops, axis=0, keepdims=True)
        sums = jnp.sum(sum_col[...] * jnp.exp2(tops - whole), axis=0, keepdims=True)
        pair_x[e, 0] = whole + jnp.log(sums) * LOG2E
        swap = swap_copy(e)
        swap.start()
        swap.wait_recv()
        col_x[e, pl.ds(chip, 1)] = log2sumexp2(pair_x[e])

        for k in range(15):
            col_copy(e, chip, k).start()
        for k in range(14, -1, -1):
            col_copy(e, row_peer(k), k).wait_recv()
        data_row[...] = -log2sumexp2(col_x[e])[0] - math.log2(8192)

    for e in range(SWEEPS):
        noise_step(e)
        noise_arrives(e)
        to_column(noise_col, -log2sumexp2(row_x[e])[0] - math.log2(16384))
        data_step(e)

    noise_step(SWEEPS)
    to_column(noise_col, row_x[SWEEPS, col])

    def transport(t, _):
        at = pl.ds(pl.multiple_of(t * group, group), group)
        for c in range(COLS // LANES):
            lanes = slice(c * LANES, (c + 1) * LANES)
            plan[at, lanes] = jnp.exp2(data_row[:, lanes] + scores[at, lanes] - noise_col[at, :]).astype(jnp.bfloat16)
        return 0

    lax.fori_loop(0, ROWS // group, transport, 0, unroll=4)

    top, low = slice(0, X_FIRST), slice(X_FIRST, ROWS)
    half = Y_FIRST // 2
    SELF, LEFT, RIGHT, MATE = range(4)

    def chunk_sum(rows, target, h):
        return jnp.dot(plan[rows, :], db[2 * target + h], preferred_element_type=jnp.float32)

    def weigh(value, who, rows):
        weight = weight_col[who, rows, :]
        return jnp.concatenate([value[:, :LANES] * weight, value[:, LANES:] * weight], axis=1)

    def fill(ref, slot, h, rows, target, add=(), weighed=True):
        value = chunk_sum(rows, target, h)
        if weighed:
            value = weigh(value, SELF, rows)
        for other, other_slot, who in add:
            term = other[other_slot, h].astype(jnp.float32)
            value = value + (term if who is None else weigh(term, who, rows))
        ref[slot, h] = value.astype(jnp.bfloat16)

    def x_copy(slot, h, to_col):
        return pltpu.make_async_remote_copy(
            x_parts.at[slot, h], x_got.at[slot, h], m_send.at[slot, h], m_recv.at[slot, h],
            device_id=(row, to_col), device_id_type=MESH)

    def y_copy(slot, h, to_col):
        return pltpu.make_async_remote_copy(
            y_parts.at[slot, h], y_got.at[slot, h], m_send.at[7 + slot, h], m_recv.at[7 + slot, h],
            device_id=(row, to_col), device_id_type=MESH)

    def y_half(which, h, to_col):
        at = pl.ds(which * half, half)
        return pltpu.make_async_remote_copy(
            y_parts.at[4, h, at, :], y_got.at[4, h, at, :], m_send.at[14 + which, h], m_recv.at[14 + which, h],
            device_id=(row, to_col), device_id_type=MESH)

    x_copies = [[x_copy(slot, h, to) for h in range(2)]
                for slot, to in enumerate((right, left, right, left, right, left, mate_col))]
    y_copies = {slot: [y_copy(slot, h, to) for h in range(2)]
                for slot, to in ((0, mate_col), (1, mate_col), (2, mate_col), (3, mate_col), (5, right), (6, left))}
    y_halves = [[y_half(which, h, to) for h in range(2)] for which, to in enumerate((right, left))]

    for h in range(2):
        fill(x_parts, 0, h, top, at_x(2), weighed=False)
        x_copies[0][h].start()
        fill(x_parts, 1, h, top, at_x(2, True), weighed=False)
        x_copies[1][h].start()
        fill(y_parts, 0, h, low, at_x(2, True), weighed=False)
        y_copies[0][h].start()
    for slot, target in ((1, at_x(1, True)), (2, at_x(-1, True)), (3, mate_col)):
        for h in range(2):
            fill(y_parts, slot, h, low, target, weighed=False)
            y_copies[slot][h].start()

    noise_arrives(SWEEPS)
    whole = log2sumexp2(row_x[SWEEPS])[0]
    for who, source in enumerate((col, left, right, mate_col)):
        to_column(weight_col.at[who], jnp.exp2(row_x[SWEEPS, source] - whole))

    for h in range(2):
        y_copies[0][h].wait_recv()
        fill(y_parts, 4, h, low, at_x(2), add=[(y_got, 0, MATE)])
        y_halves[0][h].start()
        y_halves[1][h].start()
        x_copies[1][h].wait_recv()
        fill(x_parts, 5, h, top, at_x(-1, True), add=[(x_got, 1, RIGHT)])
        x_copies[5][h].start()
        fill(x_parts, 2, h, top, at_x(1, True))
        x_copies[2][h].start()
    for h in range(2):
        x_copies[0][h].wait_recv()
        fill(x_parts, 4, h, top, right, add=[(x_got, 0, LEFT)])
        x_copies[4][h].start()
        fill(x_parts, 3, h, top, left)
        x_copies[3][h].start()

    for _, copy in sends:
        copy.wait_send()
    for e in range(SWEEPS + 1):
        for k in COL_ORDER:
            row_copy(e, col, k).wait_send()
    for e in range(SWEEPS):
        for k in range(15):
            col_copy(e, chip, k).wait_send()
        swap_copy(e).wait_send()

    def low_sum(target, h, got_slot):
        return (weigh(chunk_sum(low, target, h), SELF, low)
                + weigh(y_got[got_slot, h].astype(jnp.float32), MATE, low))

    for slot, target, got_slot, which in ((5, right, 1, 0), (6, left, 2, 1)):
        at, rest = pl.ds(which * half, half), pl.ds((1 - which) * half, half)
        for h in range(2):
            y_copies[got_slot][h].wait_recv()
            y_sum[...] = low_sum(target, h, got_slot)
            y_parts[slot, h, rest, :] = y_sum[rest, :].astype(jnp.bfloat16)
            y_halves[which][h].wait_recv()
            y_parts[slot, h, at, :] = (y_sum[at, :] + y_got[4, h, at, :].astype(jnp.float32)).astype(jnp.bfloat16)
            y_copies[slot][h].start()

    for h in range(2):
        x_copies[2][h].wait_recv()
        x_copies[5][h].wait_recv()
        fill(x_parts, 6, h, top, mate_col, add=[(x_got, 2, None), (x_got, 5, None)])
        x_copies[6][h].start()
    for h in range(2):
        lanes = slice(h * QW, (h + 1) * QW)
        y_copies[3][h].wait_recv()
        out_ref[low, lanes] = low_sum(col, h, 3)
        out_ref[top, lanes] = weigh(chunk_sum(top, col, h), SELF, top)
    for copies in x_copies[:3] + x_copies[5:6] + [y_copies[slot] for slot in range(4)] + y_halves:
        for copy in copies:
            copy.wait_send()
    for h in range(2):
        lanes = slice(h * QW, (h + 1) * QW)
        x_copies[3][h].wait_recv()
        x_copies[4][h].wait_recv()
        out_ref[top, lanes] += x_got[3, h].astype(jnp.float32) + x_got[4, h].astype(jnp.float32)
    for h in range(2):
        lanes = slice(h * QW, (h + 1) * QW)
        y_copies[5][h].wait_recv()
        y_copies[6][h].wait_recv()
        out_ref[low, lanes] += y_got[5, h].astype(jnp.float32) + y_got[6, h].astype(jnp.float32)
        x_copies[6][h].wait_recv()
        out_ref[top, lanes] += x_got[6, h].astype(jnp.float32)

    for copies in (x_copies[3], x_copies[4], x_copies[6], y_copies[5], y_copies[6]):
        for copy in copies:
            copy.wait_send()


def local(noise_latents, data_latents, flow_times):
    bf16, f32 = jnp.bfloat16, jnp.float32
    vmem, dma = pltpu.VMEM, pltpu.SemaphoreType.DMA
    matched = pl.pallas_call(
        kernel,
        out_shape=jax.ShapeDtypeStruct((ROWS, 2 * QW), f32),
        in_specs=[pl.BlockSpec(memory_space=pltpu.HBM)] * 2,
        out_specs=pl.BlockSpec(memory_space=pltpu.VMEM),
        scratch_shapes=[
            vmem((ROWS, 2 * QW), f32), vmem((COLS, LANES), f32), dma((2,)),
            vmem((QS, ROWS, QW), bf16), vmem((QS, COLS, QW), bf16), vmem((ROWS, COLS), f32), vmem((ROWS, COLS), bf16),
            vmem((7, 2, X_FIRST, QW), bf16), vmem((7, 2, X_FIRST, QW), bf16),
            vmem((7, 2, Y_FIRST, QW), bf16), vmem((7, 2, Y_FIRST, QW), bf16), vmem((Y_FIRST, QW), f32),
            vmem((ROWS, LANES), f32), vmem((ROWS, LANES), f32), vmem((ROWS, LANES), f32), vmem((4, ROWS, LANES), f32), vmem((1, COLS), f32), vmem((8, COLS), f32), vmem((8, COLS), f32),
            vmem((ROWS, LANES), f32), vmem((COLS, LANES), f32),
            vmem((SWEEPS + 1, 8, 1, ROWS), f32), vmem((SWEEPS, QS, 1, COLS), f32), vmem((SWEEPS, 2, 1, COLS), f32),
            dma((14,)), dma((8, 2)), dma((48,)), dma((16, 5)), dma((20,)), dma((16, 6)),
            dma((SWEEPS + 1, 8)), dma((SWEEPS + 1, 8)), dma((SWEEPS, 16)), dma((SWEEPS, 16)),
            dma((SWEEPS,)), dma((SWEEPS,)), dma((16, 2)), dma((16, 2)),
        ],
        compiler_params=pltpu.CompilerParams(
            collective_id=0, has_side_effects=True, vmem_limit_bytes=60 << 20),
        name="sinkhorn",
    )(noise_latents, data_latents)
    velocity = matched - noise_latents
    interpolant = noise_latents + flow_times[:, None] * velocity
    return (velocity, interpolant)


def solution(mesh):
    in_specs = (P("row", "col"), P("col", "row"), P("row"))
    out_specs = (P("row", "col"), P("row", "col"))
    return jax.shard_map(local, mesh=mesh, in_specs=in_specs, out_specs=out_specs, check_vma=False)
```

```python
import math

import jax
import jax.numpy as jnp
from jax import lax
from jax.experimental import pallas as pl
from jax.experimental.pallas import tpu as pltpu
from jax.sharding import PartitionSpec as P

D = 4096
SWEEPS = 3
entropic_epsilon = 0.02
MESH = pl.DeviceIdType.MESH
LOG2E = 1.0 / math.log(2.0)

ROWS, COLS = 512, 1024
QS, QW = 16, 256
LANES = 128
COL_ORDER = (4, 3, 5, 2, 6, 1, 7)
NEAR = ((1, 2), (1, 6), (0, 4), (1, 1), (1, 7), (0, 3), (0, 5), (1, 0), (0, 2), (0, 6), (0, 1), (0, 7))
FAR = ((1, 4), (1, 3), (1, 5))
OWN = len(NEAR)
X_FIRST = 288
Y_FIRST = ROWS - X_FIRST
SPLIT = 640
PARTS = ((0, SPLIT // 2), (SPLIT // 2, SPLIT // 2), (SPLIT, COLS - SPLIT),
         (SPLIT, (COLS - SPLIT) // 2), ((COLS + SPLIT) // 2, (COLS - SPLIT) // 2), (0, COLS))
WHOLE = 5


def log2sumexp2(values):
    largest = jnp.max(values, axis=0, keepdims=True)
    sums = jnp.sum(jnp.exp2(values - largest), axis=0, keepdims=True)
    return largest + jnp.log(sums) * LOG2E


def kernel(noise_hbm, data_hbm, out_ref,
           noise_ref, data_ref, load_sem,
           nb, db, scores, plan, x_parts, x_got, y_parts, y_got, y_sum, top_row, sum_row, noise_col, weight_col, data_row, top_col, sum_col, sq_n, sq_d,
           row_x, col_x, pair_x,
           n_send, n_recv, d_send, d_recv, s_send, s_recv,
           rx_send, rx_recv, cx_send, cx_recv, px_send, px_recv, m_send, m_recv):
    row, col = lax.axis_index("row"), lax.axis_index("col")
    yhi, z, core = row // 16, lax.rem(row // 2, 8), lax.rem(row, 2)
    x, ylo = col // 2, lax.rem(col, 2)
    chip = row // 2

    def at_x(shift, other=False):
        return lax.rem(x + shift + 4, 4) * 2 + (1 - ylo if other else ylo)

    def at_z(shift, other=False):
        return (1 - yhi if other else yhi) * 8 + lax.rem(z + shift + 8, 8)

    sibling = (row + 1 - 2 * core, col)
    load_noise = pltpu.make_async_copy(noise_hbm, noise_ref, load_sem.at[0])
    load_data = pltpu.make_async_copy(data_hbm, data_ref, load_sem.at[1])
    load_data.start()
    load_noise.start()

    up, down, mate_chip = at_z(1), at_z(-1), at_z(0, True)
    right, left, mate_col = at_x(1), at_x(-1), at_x(0, True)
    barrier = pltpu.get_barrier_semaphore()
    for peer in [sibling] + [(row, c) for c in (right, left, mate_col)] + [
            (c * 2 + core, col) for c in (up, down, mate_chip)]:
        pl.semaphore_signal(barrier, inc=1, device_id=peer, device_id_type=MESH)

    halfway = pl.ds(pl.multiple_of(core * LANES, LANES), LANES)
    load_data.wait()
    db[chip, :, halfway] = data_ref[...].astype(jnp.bfloat16)
    pl.semaphore_wait(barrier, 7)

    sends = []

    def start(kind, copy):
        copy.start()
        sends.append((kind, copy))

    def number(kind):
        return len([s for s in sends if s[0] == kind])

    def noise_copy(chunk, h, send_at, to_col):
        piece = nb.at[2 * chunk + h]
        return pltpu.make_async_remote_copy(
            piece, piece, n_send.at[send_at], n_recv.at[chunk, h], device_id=(row, to_col), device_id_type=MESH)

    def send_noise(chunk, h, *to_cols):
        for to_col in to_cols:
            start("n", noise_copy(chunk, h, number("n"), to_col))

    def wait_noise(chunk, h):
        noise_copy(chunk, h, 0, col).wait_recv()

    def data_copy(q, part, send_at, to_chip):
        first, size = PARTS[part]
        piece = db.at[q, first:first + size, halfway]
        return pltpu.make_async_remote_copy(
            piece, piece, d_send.at[send_at], d_recv.at[q, part],
            device_id=(to_chip * 2 + core, col), device_id_type=MESH)

    def send_data(q, part, *to_chips):
        for to_chip in to_chips:
            start("d", data_copy(q, part, number("d"), to_chip))

    def wait_data(q, part):
        data_copy(q, part, 0, chip).wait_recv()

    def sibling_copy(q, part, lanes, send_at):
        first, size = PARTS[part]
        piece = db.at[q, first:first + size, lanes]
        return pltpu.make_async_remote_copy(
            piece, piece, s_send.at[send_at], s_recv.at[q, part], device_id=sibling, device_id_type=MESH)

    def send_sibling(q, *parts):
        for part in parts or (WHOLE,):
            start("s", sibling_copy(q, part, halfway, number("s")))

    otherway = pl.ds(pl.multiple_of((1 - core) * LANES, LANES), LANES)

    def wait_sibling(q, *parts):
        for part in parts or (WHOLE,):
            sibling_copy(q, part, otherway, 0).wait_recv()

    def own_rest(shift):
        for q, on, end in ((at_z(-shift), up, 3), (at_z(shift), down, 4)):
            wait_data(q, 2)
            send_data(q, 2 if shift < 3 else end, on)
            send_data(q, 2, mate_chip)

    def own_data(shift):
        for part in (0, 1):
            wait_data(at_z(-shift), part)
            if shift < 3 or part == 0:
                send_data(at_z(-shift), part, up)
            wait_data(at_z(shift), part)
            if shift < 3 or part == 1:
                send_data(at_z(shift), part, down)
        send_sibling(at_z(-shift))
        send_sibling(at_z(shift))

    def mate_data(shift):
        for part in (0, 1):
            wait_data(at_z(-shift, True), part)
            if shift < 3 or part == 0:
                send_data(at_z(-shift, True), part, up)
            wait_data(at_z(shift, True), part)
            if shift < 3 or part == 1:
                send_data(at_z(shift, True), part, down)

    def mate_rest(*shifts):
        for shift in shifts:
            wait_data(at_z(shift, True), 2)
            send_sibling(at_z(shift, True))

    def data_level(q):
        ahead = lax.rem(lax.rem(q, 8) - z + 8, 8)
        far = jnp.minimum(ahead, 8 - ahead)
        return jnp.where(q // 8 == yhi, by_shift(far, (1, 2, 5, 7, 10)), by_shift(far, (3, 4, 6, 8, 10)))

    def by_shift(shift, levels):
        level = levels[-1]
        for at, value in enumerate(levels[:-1]):
            level = jnp.where(shift == at, value, level)
        return level

    def noise_level(q):
        shift, late = lax.rem(q // 4 - x + 4, 4), lax.rem(q, 2) == 1
        return jnp.where(lax.rem(q // 2, 2) == ylo, by_shift(shift, (1, 2, jnp.where(late, 6, 5), 2)),
                         by_shift(shift, (3, jnp.where(late, 6, 5), jnp.where(late, 9, 8))))

    def multiply(now):
        def block(q, _):
            @pl.when(jnp.maximum(noise_level(q), data_level(q)) == now)
            def _():
                for t in range(COLS // QW):
                    at, noise_at = slice(t * QW, (t + 1) * QW), slice(t * LANES, (t + 1) * LANES)
                    scores[:, at] += lax.dot_general(
                        nb[q], db[q, at, :], (((1,), (1,)), ((), ())), preferred_element_type=jnp.float32)
                    wide = db[q, at, :].astype(jnp.float32)
                    wide = wide * wide
                    sq_d[at, :] += wide[:, :LANES] + wide[:, LANES:]
                    wide = nb[q, noise_at, :].astype(jnp.float32)
                    wide = wide * wide
                    sq_n[noise_at, :] += wide[:, :LANES] + wide[:, LANES:]
            return 0

        lax.fori_loop(0, QS, block, 0)

    def arrive(*shifts):
        for shift in shifts:
            wait_sibling(at_z(shift))

    def mate_arrive(*shifts):
        for shift in shifts:
            wait_sibling(at_z(shift, True))

    send_data(chip, 0, mate_chip)
    send_data(chip, 1, mate_chip)
    send_data(chip, 2, up, down)
    load_noise.wait()
    for h in (0, 1):
        nb[2 * col + h] = noise_ref[:, h * QW:(h + 1) * QW].astype(jnp.bfloat16)
        send_noise(col, h, right, left, mate_col)
    send_data(chip, 0, up, down)
    send_data(chip, 1, up, down)
    send_data(chip, 2, mate_chip)
    send_sibling(chip)
    scores[...] = jnp.zeros_like(scores)
    sq_n[...] = jnp.zeros_like(sq_n)
    sq_d[...] = jnp.zeros_like(sq_d)

    own_rest(1)
    own_data(1)
    wait_noise(left, 0)
    send_noise(left, 0, right)
    wait_noise(right, 0)
    for part in (0, 1):
        wait_data(mate_chip, part)
        send_data(mate_chip, part, up, down)
    wait_noise(mate_col, 0)
    send_noise(mate_col, 0, left)
    own_rest(2)
    arrive(0)
    multiply(1)
    wait_noise(left, 1)
    send_noise(left, 1, right)
    wait_noise(right, 1)
    own_data(2)
    mate_rest(0)
    arrive(1, -1)
    multiply(2)
    wait_noise(mate_col, 1)
    send_noise(mate_col, 1, left)
    mate_data(1)
    send_noise(mate_col, 0, right)
    send_noise(mate_col, 1, right)
    own_rest(3)
    mate_rest(-1, 1)
    mate_arrive(0)
    multiply(3)
    wait_noise(at_x(1, True), 0)
    send_noise(at_x(1, True), 0, left)
    wait_noise(at_x(2), 0)
    own_data(3)
    mate_arrive(1, -1)
    multiply(4)
    mate_data(2)
    arrive(2, -2)
    multiply(5)
    wait_noise(at_x(1, True), 1)
    send_noise(at_x(1, True), 1, left)
    wait_noise(at_x(2), 1)
    mate_rest(-2, 2)
    far, far_mate = at_z(4), at_z(4, True)
    for part in (3, 4):
        wait_data(far, part)
        send_data(far, part, mate_chip)
    send_sibling(far, 2)
    mate_arrive(2, -2)
    multiply(6)
    arrive(3, -3)
    mate_data(3)
    multiply(7)
    mate_rest(-3, 3)
    wait_noise(at_x(-1, True), 0)
    wait_noise(at_x(2, True), 0)
    mate_arrive(3, -3)
    multiply(8)
    for part in (0, 1):
        wait_data(far, part)
        send_sibling(far, part)
    for part in (3, 4):
        wait_data(far_mate, part)
    send_sibling(far_mate, 2)
    for part in (0, 1):
        wait_data(far_mate, part)
        send_sibling(far_mate, part)
    wait_noise(at_x(-1, True), 1)
    wait_noise(at_x(2, True), 1)
    multiply(9)
    wait_sibling(far, 2, 0, 1)
    wait_sibling(far_mate, 2, 0, 1)
    multiply(10)

    scale = LOG2E / (entropic_epsilon * D)

    def norm_row(t, _):
        at = pl.ds(pl.multiple_of(t * LANES, LANES), LANES)
        data_row[:, at] = jnp.sum(sq_d[at, :].T, axis=0, keepdims=True)
        return 0

    lax.fori_loop(0, COLS // LANES, norm_row, 0)
    group = 32

    def to_column(column_ref, line):
        for b in range(ROWS // LANES):
            at = slice(b * LANES, (b + 1) * LANES)
            column_ref[at, :] = jnp.broadcast_to(line[:, at], (LANES, LANES)).T

    def noise_step(e):
        def pass_over(t, _):
            at = pl.ds(pl.multiple_of(t * group, group), group)
            if e == 0:
                norms = jnp.sum(sq_n[at, :], axis=1, keepdims=True)
                terms = []
                for c in range(COLS // LANES):
                    lanes = slice(c * LANES, (c + 1) * LANES)
                    terms.append((2.0 * scores[at, lanes] - norms - data_row[:, lanes]) * scale)
                    scores[at, lanes] = terms[c]
            else:
                terms = [scores[at, c * LANES:(c + 1) * LANES] + data_row[:, c * LANES:(c + 1) * LANES]
                         for c in range(COLS // LANES)]
            largest = terms[0]
            for term in terms[1:]:
                largest = jnp.maximum(largest, term)
            sums = jnp.exp2(terms[0] - largest)
            for term in terms[1:]:
                sums = sums + jnp.exp2(term - largest)
            top_row[at, :] = largest
            sum_row[at, :] = sums
            return 0
        lax.fori_loop(0, ROWS // group, pass_over, 0, unroll=4)
        for b in range(ROWS // LANES):
            at = slice(b * LANES, (b + 1) * LANES)
            tops = top_row[at, :].T
            whole = jnp.max(tops, axis=0, keepdims=True)
            sums = jnp.sum(sum_row[at, :].T * jnp.exp2(tops - whole), axis=0, keepdims=True)
            row_x[e, pl.ds(col, 1), :, at] = (whole + jnp.log(sums) * LOG2E)[None]

        for k in COL_ORDER:
            row_copy(e, col, k).start()

    def row_copy(e, source, k):
        return pltpu.make_async_remote_copy(
            row_x.at[e, source], row_x.at[e, source], rx_send.at[e, k], rx_recv.at[e, source],
            device_id=(row, lax.rem(col + k, 8)), device_id_type=MESH)

    def noise_arrives(e):
        for k in COL_ORDER[::-1]:
            row_copy(e, lax.rem(col + k, 8), k).wait_recv()

    def mirrored(peers, k):
        return peers.index((peers[k][0], (8 - peers[k][1]) % 8))

    def near_copy(e, k, slot):
        return pltpu.make_async_remote_copy(
            col_x.at[e, OWN], col_x.at[e, slot], cx_send.at[e, k], cx_recv.at[e, slot],
            device_id=(at_z(NEAR[k][1], NEAR[k][0] == 1) * 2 + core, col), device_id_type=MESH)

    def far_copy(e, k, to_core, slot, from_core):
        slot = OWN + 1 + 2 * slot + from_core
        return pltpu.make_async_remote_copy(
            pair_x.at[e, 0], col_x.at[e, slot], cx_send.at[e, OWN + 2 * k + to_core], cx_recv.at[e, slot],
            device_id=(at_z(FAR[k][1], True) * 2 + to_core, col), device_id_type=MESH)

    def row_sends(e):
        near = [near_copy(e, k, mirrored(NEAR, k)) for k in range(len(NEAR))]
        far = [far_copy(e, k, to_core, mirrored(FAR, k), core) for k in range(len(FAR)) for to_core in range(2)]
        return near, far

    def swap_copy(e):
        return pltpu.make_async_remote_copy(
            pair_x.at[e, 0], pair_x.at[e, 1], px_send.at[e], px_recv.at[e],
            device_id=sibling, device_id_type=MESH)

    def data_step(e):
        def pass_over(t, _):
            at = pl.ds(pl.multiple_of(t * LANES, LANES), LANES)
            largest, sums = [], []
            for h in range(2):
                rows = slice(h * 256, (h + 1) * 256)
                terms = (scores[rows, at] + noise_col[rows, :]).reshape(32, 8, LANES)
                largest.append(jnp.max(terms, axis=0))
                sums.append(jnp.sum(jnp.exp2(terms - largest[h][None]), axis=0))
            both = jnp.maximum(*largest)
            top_col[:, at] = both
            sum_col[:, at] = sums[0] * jnp.exp2(largest[0] - both) + sums[1] * jnp.exp2(largest[1] - both)
            return 0
        lax.fori_loop(0, COLS // LANES, pass_over, 0, unroll=4)
        tops = top_col[...]
        whole = jnp.max(tops, axis=0, keepdims=True)
        sums = jnp.sum(sum_col[...] * jnp.exp2(tops - whole), axis=0, keepdims=True)
        pair_x[e, 0] = whole + jnp.log(sums) * LOG2E
        swap, (near, far) = swap_copy(e), row_sends(e)
        swap.start()
        for copy in far:
            copy.start()
        swap.wait_recv()
        col_x[e, OWN] = log2sumexp2(pair_x[e])[0]
        for copy in near:
            copy.start()
        for k in range(len(NEAR) - 1, -1, -1):
            near_copy(e, k, k).wait_recv()
        for k in range(len(FAR)):
            for from_core in range(2):
                far_copy(e, k, 0, k, from_core).wait_recv()
        data_row[...] = -log2sumexp2(col_x[e])[0] - math.log2(8192)

    for e in range(SWEEPS):
        noise_step(e)
        noise_arrives(e)
        to_column(noise_col, -log2sumexp2(row_x[e])[0] - math.log2(16384))
        data_step(e)

    noise_step(SWEEPS)
    to_column(noise_col, row_x[SWEEPS, col])

    def transport(t, _):
        at = pl.ds(pl.multiple_of(t * group, group), group)
        for c in range(COLS // LANES):
            lanes = slice(c * LANES, (c + 1) * LANES)
            plan[at, lanes] = jnp.exp2(data_row[:, lanes] + scores[at, lanes] - noise_col[at, :]).astype(jnp.bfloat16)
        return 0

    lax.fori_loop(0, ROWS // group, transport, 0, unroll=4)

    top, low = slice(0, X_FIRST), slice(X_FIRST, ROWS)
    half = Y_FIRST // 2
    SELF, LEFT, RIGHT, MATE = range(4)

    def chunk_sum(rows, target, h):
        return jnp.dot(plan[rows, :], db[2 * target + h], preferred_element_type=jnp.float32)

    def weigh(value, who, rows):
        weight = weight_col[who, rows, :]
        return jnp.concatenate([value[:, :LANES] * weight, value[:, LANES:] * weight], axis=1)

    def fill(ref, slot, h, rows, target, add=(), weighed=True):
        value = chunk_sum(rows, target, h)
        if weighed:
            value = weigh(value, SELF, rows)
        for other, other_slot, who in add:
            term = other[other_slot, h].astype(jnp.float32)
            value = value + (term if who is None else weigh(term, who, rows))
        ref[slot, h] = value.astype(jnp.bfloat16)

    def x_copy(slot, h, to_col):
        return pltpu.make_async_remote_copy(
            x_parts.at[slot, h], x_got.at[slot, h], m_send.at[slot, h], m_recv.at[slot, h],
            device_id=(row, to_col), device_id_type=MESH)

    def y_copy(slot, h, to_col):
        return pltpu.make_async_remote_copy(
            y_parts.at[slot, h], y_got.at[slot, h], m_send.at[7 + slot, h], m_recv.at[7 + slot, h],
            device_id=(row, to_col), device_id_type=MESH)

    def y_half(which, h, to_col):
        at = pl.ds(which * half, half)
        return pltpu.make_async_remote_copy(
            y_parts.at[4, h, at, :], y_got.at[4, h, at, :], m_send.at[14 + which, h], m_recv.at[14 + which, h],
            device_id=(row, to_col), device_id_type=MESH)

    x_copies = [[x_copy(slot, h, to) for h in range(2)]
                for slot, to in enumerate((right, left, right, left, right, left, mate_col))]
    y_copies = {slot: [y_copy(slot, h, to) for h in range(2)]
                for slot, to in ((0, mate_col), (1, mate_col), (2, mate_col), (3, mate_col), (5, right), (6, left))}
    y_halves = [[y_half(which, h, to) for h in range(2)] for which, to in enumerate((right, left))]

    for h in range(2):
        fill(x_parts, 0, h, top, at_x(2), weighed=False)
        x_copies[0][h].start()
        fill(x_parts, 1, h, top, at_x(2, True), weighed=False)
        x_copies[1][h].start()
        fill(y_parts, 0, h, low, at_x(2, True), weighed=False)
        y_copies[0][h].start()
    for slot, target in ((1, at_x(1, True)), (2, at_x(-1, True)), (3, mate_col)):
        for h in range(2):
            fill(y_parts, slot, h, low, target, weighed=False)
            y_copies[slot][h].start()

    noise_arrives(SWEEPS)
    whole = log2sumexp2(row_x[SWEEPS])[0]
    for who, source in enumerate((col, left, right, mate_col)):
        to_column(weight_col.at[who], jnp.exp2(row_x[SWEEPS, source] - whole))

    for h in range(2):
        y_copies[0][h].wait_recv()
        fill(y_parts, 4, h, low, at_x(2), add=[(y_got, 0, MATE)])
        y_halves[0][h].start()
        y_halves[1][h].start()
        x_copies[1][h].wait_recv()
        fill(x_parts, 5, h, top, at_x(-1, True), add=[(x_got, 1, RIGHT)])
        x_copies[5][h].start()
        fill(x_parts, 2, h, top, at_x(1, True))
        x_copies[2][h].start()
    for h in range(2):
        x_copies[0][h].wait_recv()
        fill(x_parts, 4, h, top, right, add=[(x_got, 0, LEFT)])
        x_copies[4][h].start()
        fill(x_parts, 3, h, top, left)
        x_copies[3][h].start()

    for _, copy in sends:
        copy.wait_send()
    for e in range(SWEEPS + 1):
        for k in COL_ORDER:
            row_copy(e, col, k).wait_send()
    for e in range(SWEEPS):
        for copies in row_sends(e):
            for copy in copies:
                copy.wait_send()
        swap_copy(e).wait_send()

    def low_sum(target, h, got_slot):
        return (weigh(chunk_sum(low, target, h), SELF, low)
                + weigh(y_got[got_slot, h].astype(jnp.float32), MATE, low))

    for slot, target, got_slot, which in ((5, right, 1, 0), (6, left, 2, 1)):
        at, rest = pl.ds(which * half, half), pl.ds((1 - which) * half, half)
        for h in range(2):
            y_copies[got_slot][h].wait_recv()
            y_sum[...] = low_sum(target, h, got_slot)
            y_parts[slot, h, rest, :] = y_sum[rest, :].astype(jnp.bfloat16)
            y_halves[which][h].wait_recv()
            y_parts[slot, h, at, :] = (y_sum[at, :] + y_got[4, h, at, :].astype(jnp.float32)).astype(jnp.bfloat16)
            y_copies[slot][h].start()

    for h in range(2):
        x_copies[2][h].wait_recv()
        x_copies[5][h].wait_recv()
        fill(x_parts, 6, h, top, mate_col, add=[(x_got, 2, None), (x_got, 5, None)])
        x_copies[6][h].start()
    for h in range(2):
        lanes = slice(h * QW, (h + 1) * QW)
        y_copies[3][h].wait_recv()
        out_ref[low, lanes] = low_sum(col, h, 3)
        out_ref[top, lanes] = weigh(chunk_sum(top, col, h), SELF, top)
    for copies in x_copies[:3] + x_copies[5:6] + [y_copies[slot] for slot in range(4)] + y_halves:
        for copy in copies:
            copy.wait_send()
    for h in range(2):
        lanes = slice(h * QW, (h + 1) * QW)
        x_copies[3][h].wait_recv()
        x_copies[4][h].wait_recv()
        out_ref[top, lanes] += x_got[3, h].astype(jnp.float32) + x_got[4, h].astype(jnp.float32)
    for h in range(2):
        lanes = slice(h * QW, (h + 1) * QW)
        y_copies[5][h].wait_recv()
        y_copies[6][h].wait_recv()
        out_ref[low, lanes] += y_got[5, h].astype(jnp.float32) + y_got[6, h].astype(jnp.float32)
        x_copies[6][h].wait_recv()
        out_ref[top, lanes] += x_got[6, h].astype(jnp.float32)

    for copies in (x_copies[3], x_copies[4], x_copies[6], y_copies[5], y_copies[6]):
        for copy in copies:
            copy.wait_send()


def local(noise_latents, data_latents, flow_times):
    bf16, f32 = jnp.bfloat16, jnp.float32
    vmem, dma = pltpu.VMEM, pltpu.SemaphoreType.DMA
    matched = pl.pallas_call(
        kernel,
        out_shape=jax.ShapeDtypeStruct((ROWS, 2 * QW), f32),
        in_specs=[pl.BlockSpec(memory_space=pltpu.HBM)] * 2,
        out_specs=pl.BlockSpec(memory_space=pltpu.VMEM),
        scratch_shapes=[
            vmem((ROWS, 2 * QW), f32), vmem((COLS, LANES), f32), dma((2,)),
            vmem((QS, ROWS, QW), bf16), vmem((QS, COLS, QW), bf16), vmem((ROWS, COLS), f32), vmem((ROWS, COLS), bf16),
            vmem((7, 2, X_FIRST, QW), bf16), vmem((7, 2, X_FIRST, QW), bf16),
            vmem((7, 2, Y_FIRST, QW), bf16), vmem((7, 2, Y_FIRST, QW), bf16), vmem((Y_FIRST, QW), f32),
            vmem((ROWS, LANES), f32), vmem((ROWS, LANES), f32), vmem((ROWS, LANES), f32), vmem((4, ROWS, LANES), f32), vmem((1, COLS), f32), vmem((8, COLS), f32), vmem((8, COLS), f32),
            vmem((ROWS, LANES), f32), vmem((COLS, LANES), f32),
            vmem((SWEEPS + 1, 8, 1, ROWS), f32), vmem((SWEEPS, OWN + 1 + 2 * len(FAR), 1, COLS), f32), vmem((SWEEPS, 2, 1, COLS), f32),
            dma((14,)), dma((8, 2)), dma((48,)), dma((16, 5)), dma((20,)), dma((16, 6)),
            dma((SWEEPS + 1, 8)), dma((SWEEPS + 1, 8)), dma((SWEEPS, 20)), dma((SWEEPS, 20)),
            dma((SWEEPS,)), dma((SWEEPS,)), dma((16, 2)), dma((16, 2)),
        ],
        compiler_params=pltpu.CompilerParams(
            collective_id=0, has_side_effects=True, vmem_limit_bytes=60 << 20),
        name="sinkhorn",
    )(noise_latents, data_latents)
    velocity = matched - noise_latents
    interpolant = noise_latents + flow_times[:, None] * velocity
    return (velocity, interpolant)


def solution(mesh):
    in_specs = (P("row", "col"), P("col", "row"), P("row"))
    out_specs = (P("row", "col"), P("row", "col"))
    return jax.shard_map(local, mesh=mesh, in_specs=in_specs, out_specs=out_specs, check_vma=False)
```

```python
import math

import jax
import jax.numpy as jnp
from jax import lax
from jax.experimental import pallas as pl
from jax.experimental.pallas import tpu as pltpu
from jax.sharding import PartitionSpec as P

D = 4096
SWEEPS = 3
entropic_epsilon = 0.02
MESH = pl.DeviceIdType.MESH
LOG2E = 1.0 / math.log(2.0)

ROWS, COLS = 512, 1024
QS, QW = 16, 256
LANES = 128
COL_ORDER = (4, 3, 5, 2, 6, 1, 7)
NEAR = ((1, 2), (1, 6), (0, 4), (1, 1), (1, 7), (0, 3), (0, 5), (1, 0), (0, 2), (0, 6), (0, 1), (0, 7))
FAR = ((1, 4), (1, 3), (1, 5))
OWN = len(NEAR)
X_FIRST = 288
Y_FIRST = ROWS - X_FIRST
SPLIT = 640
PARTS = ((0, SPLIT // 2), (SPLIT // 2, SPLIT // 2), (SPLIT, COLS - SPLIT),
         (SPLIT, (COLS - SPLIT) // 2), ((COLS + SPLIT) // 2, (COLS - SPLIT) // 2), (0, COLS))
WHOLE = 5


def log2sumexp2(values):
    largest = jnp.max(values, axis=0, keepdims=True)
    sums = jnp.sum(jnp.exp2(values - largest), axis=0, keepdims=True)
    return largest + jnp.log(sums) * LOG2E


def kernel(noise_hbm, data_hbm, out_ref,
           noise_ref, data_ref, load_sem,
           nb, db, scores, plan, x_parts, x_got, y_parts, y_got, y_sum, top_row, sum_row, noise_col, weight_col, data_row, top_col, sum_col, sq_n, sq_d,
           row_x, col_x, pair_x,
           n_send, n_recv, d_send, d_recv, s_send, s_recv,
           rx_send, rx_recv, cx_send, cx_recv, px_send, px_recv, m_send, m_recv):
    row, col = lax.axis_index("row"), lax.axis_index("col")
    yhi, z, core = row // 16, lax.rem(row // 2, 8), lax.rem(row, 2)
    x, ylo = col // 2, lax.rem(col, 2)
    chip = row // 2

    def at_x(shift, other=False):
        return lax.rem(x + shift + 4, 4) * 2 + (1 - ylo if other else ylo)

    def at_z(shift, other=False):
        return (1 - yhi if other else yhi) * 8 + lax.rem(z + shift + 8, 8)

    sibling = (row + 1 - 2 * core, col)
    load_noise = pltpu.make_async_copy(noise_hbm, noise_ref, load_sem.at[0])
    load_data = pltpu.make_async_copy(data_hbm, data_ref, load_sem.at[1])
    load_data.start()
    load_noise.start()

    up, down, mate_chip = at_z(1), at_z(-1), at_z(0, True)
    right, left, mate_col = at_x(1), at_x(-1), at_x(0, True)
    barrier = pltpu.get_barrier_semaphore()
    for peer in [sibling] + [(row, c) for c in (right, left, mate_col)] + [
            (c * 2 + core, col) for c in (up, down, mate_chip)]:
        pl.semaphore_signal(barrier, inc=1, device_id=peer, device_id_type=MESH)

    halfway = pl.ds(pl.multiple_of(core * LANES, LANES), LANES)
    load_data.wait()
    db[chip, :, halfway] = data_ref[...].astype(jnp.bfloat16)
    pl.semaphore_wait(barrier, 7)

    sends = []

    def start(kind, copy):
        copy.start()
        sends.append((kind, copy))

    def number(kind):
        return len([s for s in sends if s[0] == kind])

    def noise_copy(chunk, h, send_at, to_col):
        piece = nb.at[2 * chunk + h]
        return pltpu.make_async_remote_copy(
            piece, piece, n_send.at[send_at], n_recv.at[chunk, h], device_id=(row, to_col), device_id_type=MESH)

    def send_noise(chunk, h, *to_cols):
        for to_col in to_cols:
            start("n", noise_copy(chunk, h, number("n"), to_col))

    def wait_noise(chunk, h):
        noise_copy(chunk, h, 0, col).wait_recv()

    def data_copy(q, part, send_at, to_chip):
        first, size = PARTS[part]
        piece = db.at[q, first:first + size, halfway]
        return pltpu.make_async_remote_copy(
            piece, piece, d_send.at[send_at], d_recv.at[q, part],
            device_id=(to_chip * 2 + core, col), device_id_type=MESH)

    def send_data(q, part, *to_chips):
        for to_chip in to_chips:
            start("d", data_copy(q, part, number("d"), to_chip))

    def wait_data(q, part):
        data_copy(q, part, 0, chip).wait_recv()

    def sibling_copy(q, part, lanes, send_at):
        first, size = PARTS[part]
        piece = db.at[q, first:first + size, lanes]
        return pltpu.make_async_remote_copy(
            piece, piece, s_send.at[send_at], s_recv.at[q, part], device_id=sibling, device_id_type=MESH)

    def send_sibling(q, *parts):
        for part in parts or (WHOLE,):
            start("s", sibling_copy(q, part, halfway, number("s")))

    otherway = pl.ds(pl.multiple_of((1 - core) * LANES, LANES), LANES)

    def wait_sibling(q, *parts):
        for part in parts or (WHOLE,):
            sibling_copy(q, part, otherway, 0).wait_recv()

    def own_rest(shift):
        for q, on, end in ((at_z(-shift), up, 3), (at_z(shift), down, 4)):
            wait_data(q, 2)
            send_data(q, 2 if shift < 3 else end, on)
            send_data(q, 2, mate_chip)

    def own_data(shift):
        for part in (0, 1):
            wait_data(at_z(-shift), part)
            if shift < 3 or part == 0:
                send_data(at_z(-shift), part, up)
            wait_data(at_z(shift), part)
            if shift < 3 or part == 1:
                send_data(at_z(shift), part, down)
        send_sibling(at_z(-shift))
        send_sibling(at_z(shift))

    def mate_data(shift):
        for part in (0, 1):
            wait_data(at_z(-shift, True), part)
            if shift < 3 or part == 0:
                send_data(at_z(-shift, True), part, up)
            wait_data(at_z(shift, True), part)
            if shift < 3 or part == 1:
                send_data(at_z(shift, True), part, down)

    def mate_rest(*shifts):
        for shift in shifts:
            wait_data(at_z(shift, True), 2)
            send_sibling(at_z(shift, True))

    def data_level(q):
        ahead = lax.rem(lax.rem(q, 8) - z + 8, 8)
        far = jnp.minimum(ahead, 8 - ahead)
        return jnp.where(q // 8 == yhi, by_shift(far, (1, 2, 5, 7, 10)), by_shift(far, (3, 4, 6, 8, 10)))

    def by_shift(shift, levels):
        level = levels[-1]
        for at, value in enumerate(levels[:-1]):
            level = jnp.where(shift == at, value, level)
        return level

    def noise_level(q):
        shift, late = lax.rem(q // 4 - x + 4, 4), lax.rem(q, 2) == 1
        return jnp.where(lax.rem(q // 2, 2) == ylo, by_shift(shift, (1, 2, jnp.where(late, 6, 5), 2)),
                         by_shift(shift, (3, jnp.where(late, 6, 5), jnp.where(late, 9, 8))))

    def add_blocks(*qs):
        for t in range(COLS // QW):
            at, noise_at = slice(t * QW, (t + 1) * QW), slice(t * LANES, (t + 1) * LANES)
            total, data_squares, noise_squares = scores[:, at], sq_d[at, :], sq_n[noise_at, :]
            for q in qs:
                total += lax.dot_general(
                    nb[q], db[q, at, :], (((1,), (1,)), ((), ())), preferred_element_type=jnp.float32)
                wide = db[q, at, :].astype(jnp.float32)
                wide = wide * wide
                data_squares = data_squares + (wide[:, :LANES] + wide[:, LANES:])
                wide = nb[q, noise_at, :].astype(jnp.float32)
                wide = wide * wide
                noise_squares = noise_squares + (wide[:, :LANES] + wide[:, LANES:])
            scores[:, at], sq_d[at, :], sq_n[noise_at, :] = total, data_squares, noise_squares

    def multiply(now):
        def block(q, _):
            pl.when(jnp.maximum(noise_level(q), data_level(q)) == now)(lambda: add_blocks(q))
            return 0

        lax.fori_loop(0, QS, block, 0)

    def arrive(*shifts):
        for shift in shifts:
            wait_sibling(at_z(shift))

    def mate_arrive(*shifts):
        for shift in shifts:
            wait_sibling(at_z(shift, True))

    send_data(chip, 0, mate_chip)
    send_data(chip, 1, mate_chip)
    send_data(chip, 2, up, down)
    load_noise.wait()
    for h in (0, 1):
        nb[2 * col + h] = noise_ref[:, h * QW:(h + 1) * QW].astype(jnp.bfloat16)
        send_noise(col, h, right, left, mate_col)
    send_data(chip, 0, up, down)
    send_data(chip, 1, up, down)
    send_data(chip, 2, mate_chip)
    send_sibling(chip)
    scores[...] = jnp.zeros_like(scores)
    sq_n[...] = jnp.zeros_like(sq_n)
    sq_d[...] = jnp.zeros_like(sq_d)

    own_rest(1)
    own_data(1)
    wait_noise(left, 0)
    send_noise(left, 0, right)
    wait_noise(right, 0)
    for part in (0, 1):
        wait_data(mate_chip, part)
        send_data(mate_chip, part, up, down)
    wait_noise(mate_col, 0)
    send_noise(mate_col, 0, left)
    own_rest(2)
    arrive(0)
    multiply(1)
    wait_noise(left, 1)
    send_noise(left, 1, right)
    wait_noise(right, 1)
    own_data(2)
    mate_rest(0)
    arrive(1, -1)
    multiply(2)
    wait_noise(mate_col, 1)
    send_noise(mate_col, 1, left)
    mate_data(1)
    send_noise(mate_col, 0, right)
    send_noise(mate_col, 1, right)
    own_rest(3)
    mate_rest(-1, 1)
    mate_arrive(0)
    multiply(3)
    wait_noise(at_x(1, True), 0)
    send_noise(at_x(1, True), 0, left)
    wait_noise(at_x(2), 0)
    own_data(3)
    mate_arrive(1, -1)
    multiply(4)
    mate_data(2)
    arrive(2, -2)
    multiply(5)
    wait_noise(at_x(1, True), 1)
    send_noise(at_x(1, True), 1, left)
    wait_noise(at_x(2), 1)
    mate_rest(-2, 2)
    far, far_mate = at_z(4), at_z(4, True)
    for part in (3, 4):
        wait_data(far, part)
        send_data(far, part, mate_chip)
    send_sibling(far, 2)
    mate_arrive(2, -2)
    multiply(6)
    arrive(3, -3)
    mate_data(3)
    multiply(7)
    mate_rest(-3, 3)
    wait_noise(at_x(-1, True), 0)
    wait_noise(at_x(2, True), 0)
    mate_arrive(3, -3)
    multiply(8)
    for part in (0, 1):
        wait_data(far, part)
        send_sibling(far, part)
    for part in (3, 4):
        wait_data(far_mate, part)
    send_sibling(far_mate, 2)
    for part in (0, 1):
        wait_data(far_mate, part)
        send_sibling(far_mate, part)
    wait_noise(at_x(-1, True), 1)
    wait_noise(at_x(2, True), 1)
    multiply(9)
    wait_sibling(far, 2, 0, 1)
    wait_sibling(far_mate, 2, 0, 1)
    add_blocks(far, far_mate)

    scale = LOG2E / (entropic_epsilon * D)

    def norm_row(t, _):
        at = pl.ds(pl.multiple_of(t * LANES, LANES), LANES)
        data_row[:, at] = jnp.sum(sq_d[at, :].T, axis=0, keepdims=True)
        return 0

    lax.fori_loop(0, COLS // LANES, norm_row, 0, unroll=4)
    group = 32

    def to_column(column_ref, line):
        for b in range(ROWS // LANES):
            at = slice(b * LANES, (b + 1) * LANES)
            column_ref[at, :] = jnp.broadcast_to(line[:, at], (LANES, LANES)).T

    def noise_step(e):
        def pass_over(t, _):
            at = pl.ds(pl.multiple_of(t * group, group), group)
            if e == 0:
                norms = jnp.sum(sq_n[at, :], axis=1, keepdims=True)
                terms = []
                for c in range(COLS // LANES):
                    lanes = slice(c * LANES, (c + 1) * LANES)
                    terms.append((2.0 * scores[at, lanes] - norms - data_row[:, lanes]) * scale)
                    scores[at, lanes] = terms[c]
            else:
                terms = [scores[at, c * LANES:(c + 1) * LANES] + data_row[:, c * LANES:(c + 1) * LANES]
                         for c in range(COLS // LANES)]
            largest = terms[0]
            for term in terms[1:]:
                largest = jnp.maximum(largest, term)
            sums = jnp.exp2(terms[0] - largest)
            for term in terms[1:]:
                sums = sums + jnp.exp2(term - largest)
            top_row[at, :] = largest
            sum_row[at, :] = sums
            return 0
        lax.fori_loop(0, ROWS // group, pass_over, 0, unroll=4)
        for b in range(ROWS // LANES):
            at = slice(b * LANES, (b + 1) * LANES)
            tops = top_row[at, :].T
            whole = jnp.max(tops, axis=0, keepdims=True)
            sums = jnp.sum(sum_row[at, :].T * jnp.exp2(tops - whole), axis=0, keepdims=True)
            row_x[e, pl.ds(col, 1), :, at] = (whole + jnp.log(sums) * LOG2E)[None]

        for k in COL_ORDER:
            row_copy(e, col, k).start()

    def row_copy(e, source, k):
        return pltpu.make_async_remote_copy(
            row_x.at[e, source], row_x.at[e, source], rx_send.at[e, k], rx_recv.at[e, source],
            device_id=(row, lax.rem(col + k, 8)), device_id_type=MESH)

    def noise_arrives(e):
        for k in COL_ORDER[::-1]:
            row_copy(e, lax.rem(col + k, 8), k).wait_recv()

    def mirrored(peers, k):
        return peers.index((peers[k][0], (8 - peers[k][1]) % 8))

    def near_copy(e, k, slot):
        return pltpu.make_async_remote_copy(
            col_x.at[e, OWN], col_x.at[e, slot], cx_send.at[e, k], cx_recv.at[e, slot],
            device_id=(at_z(NEAR[k][1], NEAR[k][0] == 1) * 2 + core, col), device_id_type=MESH)

    def far_copy(e, k, to_core, slot, from_core):
        slot = OWN + 1 + 2 * slot + from_core
        return pltpu.make_async_remote_copy(
            pair_x.at[e, 0], col_x.at[e, slot], cx_send.at[e, OWN + 2 * k + to_core], cx_recv.at[e, slot],
            device_id=(at_z(FAR[k][1], True) * 2 + to_core, col), device_id_type=MESH)

    def row_sends(e):
        near = [near_copy(e, k, mirrored(NEAR, k)) for k in range(len(NEAR))]
        far = [far_copy(e, k, to_core, mirrored(FAR, k), core) for k in range(len(FAR)) for to_core in range(2)]
        return near, far

    def swap_copy(e):
        return pltpu.make_async_remote_copy(
            pair_x.at[e, 0], pair_x.at[e, 1], px_send.at[e], px_recv.at[e],
            device_id=sibling, device_id_type=MESH)

    def data_step(e):
        def pass_over(t, _):
            at = pl.ds(pl.multiple_of(t * LANES, LANES), LANES)
            largest, sums = [], []
            for h in range(2):
                rows = slice(h * 256, (h + 1) * 256)
                terms = (scores[rows, at] + noise_col[rows, :]).reshape(32, 8, LANES)
                largest.append(jnp.max(terms, axis=0))
                sums.append(jnp.sum(jnp.exp2(terms - largest[h][None]), axis=0))
            both = jnp.maximum(*largest)
            top_col[:, at] = both
            sum_col[:, at] = sums[0] * jnp.exp2(largest[0] - both) + sums[1] * jnp.exp2(largest[1] - both)
            return 0
        lax.fori_loop(0, COLS // LANES, pass_over, 0, unroll=4)
        tops = top_col[...]
        whole = jnp.max(tops, axis=0, keepdims=True)
        sums = jnp.sum(sum_col[...] * jnp.exp2(tops - whole), axis=0, keepdims=True)
        pair_x[e, 0] = whole + jnp.log(sums) * LOG2E
        swap, (near, far) = swap_copy(e), row_sends(e)
        swap.start()
        for copy in far:
            copy.start()
        swap.wait_recv()
        col_x[e, OWN] = log2sumexp2(pair_x[e])[0]
        for copy in near:
            copy.start()
        for k in range(len(NEAR) - 1, -1, -1):
            near_copy(e, k, k).wait_recv()
        for k in range(len(FAR)):
            for from_core in range(2):
                far_copy(e, k, 0, k, from_core).wait_recv()
        data_row[...] = -log2sumexp2(col_x[e])[0] - math.log2(8192)

    for e in range(SWEEPS):
        noise_step(e)
        noise_arrives(e)
        to_column(noise_col, -log2sumexp2(row_x[e])[0] - math.log2(16384))
        data_step(e)

    noise_step(SWEEPS)
    to_column(noise_col, row_x[SWEEPS, col])

    def transport(t, _):
        at = pl.ds(pl.multiple_of(t * group, group), group)
        for c in range(COLS // LANES):
            lanes = slice(c * LANES, (c + 1) * LANES)
            plan[at, lanes] = jnp.exp2(data_row[:, lanes] + scores[at, lanes] - noise_col[at, :]).astype(jnp.bfloat16)
        return 0

    lax.fori_loop(0, ROWS // group, transport, 0, unroll=4)

    top, low = slice(0, X_FIRST), slice(X_FIRST, ROWS)
    half = Y_FIRST // 2
    SELF, LEFT, RIGHT, MATE = range(4)

    def chunk_sum(rows, target, h):
        return jnp.dot(plan[rows, :], db[2 * target + h], preferred_element_type=jnp.float32)

    def weigh(value, who, rows):
        weight = weight_col[who, rows, :]
        return jnp.concatenate([value[:, :LANES] * weight, value[:, LANES:] * weight], axis=1)

    def fill(ref, slot, h, rows, target, add=(), weighed=True):
        value = chunk_sum(rows, target, h)
        if weighed:
            value = weigh(value, SELF, rows)
        for other, other_slot, who in add:
            term = other[other_slot, h].astype(jnp.float32)
            value = value + (term if who is None else weigh(term, who, rows))
        ref[slot, h] = value.astype(jnp.bfloat16)

    def x_copy(slot, h, to_col):
        return pltpu.make_async_remote_copy(
            x_parts.at[slot, h], x_got.at[slot, h], m_send.at[slot, h], m_recv.at[slot, h],
            device_id=(row, to_col), device_id_type=MESH)

    def y_copy(slot, h, to_col):
        return pltpu.make_async_remote_copy(
            y_parts.at[slot, h], y_got.at[slot, h], m_send.at[7 + slot, h], m_recv.at[7 + slot, h],
            device_id=(row, to_col), device_id_type=MESH)

    def y_half(which, h, to_col):
        at = pl.ds(which * half, half)
        return pltpu.make_async_remote_copy(
            y_parts.at[4, h, at, :], y_got.at[4, h, at, :], m_send.at[14 + which, h], m_recv.at[14 + which, h],
            device_id=(row, to_col), device_id_type=MESH)

    x_copies = [[x_copy(slot, h, to) for h in range(2)]
                for slot, to in enumerate((right, left, right, left, right, left, mate_col))]
    y_copies = {slot: [y_copy(slot, h, to) for h in range(2)]
                for slot, to in ((0, mate_col), (1, mate_col), (2, mate_col), (3, mate_col), (5, right), (6, left))}
    y_halves = [[y_half(which, h, to) for h in range(2)] for which, to in enumerate((right, left))]

    for h in range(2):
        fill(x_parts, 0, h, top, at_x(2), weighed=False)
        x_copies[0][h].start()
        fill(x_parts, 1, h, top, at_x(2, True), weighed=False)
        x_copies[1][h].start()
        fill(y_parts, 0, h, low, at_x(2, True), weighed=False)
        y_copies[0][h].start()
    for slot, target in ((1, at_x(1, True)), (2, at_x(-1, True)), (3, mate_col)):
        for h in range(2):
            fill(y_parts, slot, h, low, target, weighed=False)
            y_copies[slot][h].start()

    noise_arrives(SWEEPS)
    whole = log2sumexp2(row_x[SWEEPS])[0]
    for who, source in enumerate((col, left, right, mate_col)):
        to_column(weight_col.at[who], jnp.exp2(row_x[SWEEPS, source] - whole))

    for h in range(2):
        y_copies[0][h].wait_recv()
        fill(y_parts, 4, h, low, at_x(2), add=[(y_got, 0, MATE)])
        y_halves[0][h].start()
        y_halves[1][h].start()
        x_copies[1][h].wait_recv()
        fill(x_parts, 5, h, top, at_x(-1, True), add=[(x_got, 1, RIGHT)])
        x_copies[5][h].start()
        fill(x_parts, 2, h, top, at_x(1, True))
        x_copies[2][h].start()
    for h in range(2):
        x_copies[0][h].wait_recv()
        fill(x_parts, 4, h, top, right, add=[(x_got, 0, LEFT)])
        x_copies[4][h].start()
        fill(x_parts, 3, h, top, left)
        x_copies[3][h].start()

    for _, copy in sends:
        copy.wait_send()
    for e in range(SWEEPS + 1):
        for k in COL_ORDER:
            row_copy(e, col, k).wait_send()
    for e in range(SWEEPS):
        for copies in row_sends(e):
            for copy in copies:
                copy.wait_send()
        swap_copy(e).wait_send()

    def low_sum(target, h, got_slot):
        return (weigh(chunk_sum(low, target, h), SELF, low)
                + weigh(y_got[got_slot, h].astype(jnp.float32), MATE, low))

    for slot, target, got_slot, which in ((5, right, 1, 0), (6, left, 2, 1)):
        at, rest = pl.ds(which * half, half), pl.ds((1 - which) * half, half)
        for h in range(2):
            y_copies[got_slot][h].wait_recv()
            y_sum[...] = low_sum(target, h, got_slot)
            y_parts[slot, h, rest, :] = y_sum[rest, :].astype(jnp.bfloat16)
            y_halves[which][h].wait_recv()
            y_parts[slot, h, at, :] = (y_sum[at, :] + y_got[4, h, at, :].astype(jnp.float32)).astype(jnp.bfloat16)
            y_copies[slot][h].start()

    for h in range(2):
        x_copies[2][h].wait_recv()
        x_copies[5][h].wait_recv()
        fill(x_parts, 6, h, top, mate_col, add=[(x_got, 2, None), (x_got, 5, None)])
        x_copies[6][h].start()
    for h in range(2):
        lanes = slice(h * QW, (h + 1) * QW)
        y_copies[3][h].wait_recv()
        out_ref[low, lanes] = low_sum(col, h, 3)
        out_ref[top, lanes] = weigh(chunk_sum(top, col, h), SELF, top)
    for copies in x_copies[:3] + x_copies[5:6] + [y_copies[slot] for slot in range(4)] + y_halves:
        for copy in copies:
            copy.wait_send()
    for h in range(2):
        lanes = slice(h * QW, (h + 1) * QW)
        x_copies[3][h].wait_recv()
        x_copies[4][h].wait_recv()
        out_ref[top, lanes] += x_got[3, h].astype(jnp.float32) + x_got[4, h].astype(jnp.float32)
    for h in range(2):
        lanes = slice(h * QW, (h + 1) * QW)
        y_copies[5][h].wait_recv()
        y_copies[6][h].wait_recv()
        out_ref[low, lanes] += y_got[5, h].astype(jnp.float32) + y_got[6, h].astype(jnp.float32)
        x_copies[6][h].wait_recv()
        out_ref[top, lanes] += x_got[6, h].astype(jnp.float32)

    for copies in (x_copies[3], x_copies[4], x_copies[6], y_copies[5], y_copies[6]):
        for copy in copies:
            copy.wait_send()


def local(noise_latents, data_latents, flow_times):
    bf16, f32 = jnp.bfloat16, jnp.float32
    vmem, dma = pltpu.VMEM, pltpu.SemaphoreType.DMA
    matched = pl.pallas_call(
        kernel,
        out_shape=jax.ShapeDtypeStruct((ROWS, 2 * QW), f32),
        in_specs=[pl.BlockSpec(memory_space=pltpu.HBM)] * 2,
        out_specs=pl.BlockSpec(memory_space=pltpu.VMEM),
        scratch_shapes=[
            vmem((ROWS, 2 * QW), f32), vmem((COLS, LANES), f32), dma((2,)),
            vmem((QS, ROWS, QW), bf16), vmem((QS, COLS, QW), bf16), vmem((ROWS, COLS), f32), vmem((ROWS, COLS), bf16),
            vmem((7, 2, X_FIRST, QW), bf16), vmem((7, 2, X_FIRST, QW), bf16),
            vmem((7, 2, Y_FIRST, QW), bf16), vmem((7, 2, Y_FIRST, QW), bf16), vmem((Y_FIRST, QW), f32),
            vmem((ROWS, LANES), f32), vmem((ROWS, LANES), f32), vmem((ROWS, LANES), f32), vmem((4, ROWS, LANES), f32), vmem((1, COLS), f32), vmem((8, COLS), f32), vmem((8, COLS), f32),
            vmem((ROWS, LANES), f32), vmem((COLS, LANES), f32),
            vmem((SWEEPS + 1, 8, 1, ROWS), f32), vmem((SWEEPS, OWN + 1 + 2 * len(FAR), 1, COLS), f32), vmem((SWEEPS, 2, 1, COLS), f32),
            dma((14,)), dma((8, 2)), dma((48,)), dma((16, 5)), dma((20,)), dma((16, 6)),
            dma((SWEEPS + 1, 8)), dma((SWEEPS + 1, 8)), dma((SWEEPS, 20)), dma((SWEEPS, 20)),
            dma((SWEEPS,)), dma((SWEEPS,)), dma((16, 2)), dma((16, 2)),
        ],
        compiler_params=pltpu.CompilerParams(
            collective_id=0, has_side_effects=True, vmem_limit_bytes=60 << 20),
        name="sinkhorn",
    )(noise_latents, data_latents)
    velocity = matched - noise_latents
    interpolant = noise_latents + flow_times[:, None] * velocity
    return (velocity, interpolant)


def solution(mesh):
    in_specs = (P("row", "col"), P("col", "row"), P("row"))
    out_specs = (P("row", "col"), P("row", "col"))
    return jax.shard_map(local, mesh=mesh, in_specs=in_specs, out_specs=out_specs, check_vma=False)
```
